32 devices in a mesh: dp: 16 (over z, y, x), grp: 2 (over core).
Axes of the slice: x: 2, y: 2, z: 4, core: 2. Of those that a mesh axis runs over, the one named last changes fastest.
Arguments:
- audio: bfloat16 [384, 232, 320], P(('dp', 'grp')), may hold values from -3 to 3
- lengths: int32 [384], P('dp'), may hold values from 37 to 225, as said below
- codes: int32 [2, 2, 384, 232], P(None, None, 'dp'), may hold values from 0 to 1023
- disc_weight: bfloat16 [960, 512], replicated, may hold values from -0.1875 to 0.1875
- disc_score: float32 [512], replicated, may hold values from -0.25 to 0.25
- params: float32 [1441792], P('dp')
- params_mom: float32 [1441792], P('dp'), may hold values from -0.0009765625 to 0.0009765625
- params_avg: float32 [1441792], P('dp')
- books: float32 [2, 524288], P('grp', 'dp'), may hold values from -4 to 4
- books_mom: float32 [2, 524288], P('grp', 'dp'), may hold values from -3.8146973e-05 to 3.8146973e-05
- books_avg: float32 [2, 524288], P('grp', 'dp'), may hold values from -4 to 4
Outputs:
- params_new: float32 [1441792], P('dp')
- params_mom_new: float32 [1441792], P('dp')
- params_avg_new: float32 [1441792], P('dp')
- books_new: float32 [2, 524288], P('grp', 'dp')
- books_mom_new: float32 [2, 524288], P('grp', 'dp')
- books_avg_new: float32 [2, 524288], P('grp', 'dp')
- loss_sum: float32 [], replicated
- frame_count: float32 [], replicated
The draws below stay inside these ranges and needn't reach their ends.
Inputs may be any that keep to these rules, and one draw needn't show every extreme that they name: lengths of the clips; 225 is reached in every draw.
All inputs are finite; a program needn't handle non-finite values.
Results may differ from the reference program's by a relative error of at most 0.0024.
Values may be sent and summed in bfloat16 or wider, within the bound.
A program may use at most 192 MiB of HBM per device.

```python
import math
import jax
import jax.numpy as jnp
from jax import lax

HOP = 320
D = 512
CB = 1024
GROUPS = 2
LEVELS = 2
KS = 3
SLOT = 232
CLIP_DEV = 12
GD = 256
CLIPS = 384
P_SIZE = 1441792
BOOK = 524288


def draw_lengths(key, part):
    key = jax.random.fold_in(key, 5)
    first_key, second_key = jax.random.split(key)
    indices = jnp.arange(CLIPS)
    owners = indices // CLIP_DEV
    devices_n = CLIPS // CLIP_DEV
    lowest = 37 + 133 * owners // (devices_n - 1)
    highest = 96 + 129 * owners // (devices_n - 1)
    drawn = jax.random.randint(first_key, (CLIPS,), lowest, highest)
    chosen = jax.random.randint(second_key, (), 0, CLIPS)
    return jnp.where(indices == chosen, 225, drawn).astype(jnp.int32)


def shaped_weights(key):
    spots = jnp.arange(P_SIZE)
    fan_inputs = jnp.where(spots < KS * HOP * D, KS * HOP, jnp.where(spots < KS * HOP * D + KS * D * D, KS * D, D))
    values = jax.random.normal(key, (P_SIZE,), jnp.float32)
    return values / jnp.sqrt(fan_inputs.astype(jnp.float32))


def draw_params(key, part):
    key = jax.random.fold_in(key, 11)
    return shaped_weights(key)


def draw_params_avg(key, part):
    key = jax.random.fold_in(key, 12)
    return shaped_weights(key)


def set_ends(entries, key, smallest, high):
    longest = entries.shape.index(max(entries.shape))
    spots = []
    for shift in (0, 1):
        where = [jax.random.randint(jax.random.fold_in(key, axis), (), 0, length) for axis, length in enumerate(entries.shape)]
        where[longest] = (where[longest] + shift) % entries.shape[longest]
        spots.append(tuple(where))
    return entries.at[spots[0]].set(smallest).at[spots[1]].set(high)


def levels(key, extent, cuts, smallest, high):
    level, own = 1.0, jax.random.fold_in(key, 6)
    for axis_at, blocks in cuts:
        draws = jnp.exp(jax.random.uniform(jax.random.fold_in(own, axis_at), (blocks,), jnp.float32, smallest / len(cuts), high / len(cuts)))
        level = level * jnp.repeat(draws, extent[axis_at] // blocks).reshape([-1 if axis == axis_at else 1 for axis in range(len(extent))])
    return level


def gaussian(own_key, dims, deviation, limit, shards=(), kind=jnp.bfloat16):
    factor_of = levels(own_key, dims, shards, -0.22, 0.18) if shards else 1.0
    values = jax.random.normal(own_key, dims, jnp.float32) * deviation * factor_of
    return jnp.minimum(jnp.maximum(values, -limit), limit).astype(kind)


def setup_inputs(seed: int = 0) -> dict:
    splits = jax.random.split(jax.random.key(seed), 12)
    audio = gaussian(splits[0], (CLIPS, SLOT, HOP), 0.5, 3.0, ((0, 32),))
    lengths = draw_lengths(jax.random.fold_in(splits[11], 71), 0)
    codes = set_ends(jax.random.randint(splits[2], (GROUPS, LEVELS, CLIPS, SLOT), 0, CB), jax.random.fold_in(splits[2], 1), 0, CB - 1).astype(jnp.int32)
    disc_weight = gaussian(splits[3], (KS * HOP, D), (KS * HOP) ** -0.5, 0.1875)
    disc_score = gaussian(splits[4], (D,), D ** -0.5, 0.25, (), jnp.float32)
    params = draw_params(jax.random.fold_in(splits[11], 71), 0)
    params_mom = gaussian(splits[6], (P_SIZE,), (0.015 / (131 * CLIPS) ** 0.5), 0.0009765625, ((0, 16),), jnp.float32)
    params_avg = draw_params_avg(jax.random.fold_in(splits[11], 71), 0)
    books = gaussian(splits[8], (GROUPS, BOOK), 0.7, 4.0, ((0, 2), (1, 16)), jnp.float32)
    books_mom = gaussian(splits[9], (GROUPS, BOOK), (0.02 / (131 * CLIPS * CB) ** 0.5), 3.814697265625e-05, ((0, 2), (1, 16)), jnp.float32)
    books_avg = gaussian(splits[10], (GROUPS, BOOK), 0.7, 4.0, ((0, 2), (1, 16)), jnp.float32)
    return dict(audio=audio, lengths=lengths, codes=codes, disc_weight=disc_weight, disc_score=disc_score, params=params, params_mom=params_mom, params_avg=params_avg, books=books, books_mom=books_mom, books_avg=books_avg)


@jax.custom_vjp
def low(v):
    return lax.optimization_barrier(v.astype(jnp.bfloat16)).astype(jnp.float32)

@jax.custom_vjp
def low_back(v):
    return v

def low_keep(v):
    return (low(v), None)

def low_pass(kept, grad):
    return (grad,)

def back_keep(v):
    return (v, None)

def back_low(kept, grad):
    return (low(grad),)
low.defvjp(low_keep, low_pass)
low_back.defvjp(back_keep, back_low)
MOMENTUM = 0.9
AVERAGE = 0.99

def spectral_table(samples):
    spots = jnp.arange(samples, dtype=jnp.int32)[:, None]
    bins = jnp.arange(samples // 2, dtype=jnp.int32)[None, :]
    turns = (spots * bins % samples).astype(jnp.float32) * (2.0 * math.pi / samples)
    window = 0.5 - 0.5 * jnp.cos((spots.astype(jnp.float32) + 0.5) * (2.0 * math.pi / samples))
    scale = math.sqrt(2.0 / samples)
    return jnp.concatenate([window * jnp.cos(turns), window * jnp.sin(turns)], axis=1) * scale

def stack_three(values):
    padded = jnp.pad(values, ((0, 0), (1, 1), (0, 0)))
    return jnp.concatenate([padded[:, :-2], padded[:, 1:-1], padded[:, 2:]], axis=2)

def high_dot(operand, weights):
    return jnp.einsum('bsk,kd->bsd', operand, weights, precision=lax.Precision.HIGHEST)

def smooth_cost(values):
    return jnp.sqrt(values * values + 1.0) - 1.0

def magnitude(spectrum):
    half = spectrum.shape[-1] // 2
    real_part = spectrum[..., :half]
    imag_part = spectrum[..., half:]
    return jnp.sqrt(real_part * real_part + imag_part * imag_part + 1.0)

def split_weights(shared):
    enc_size = KS * HOP * D
    dec_size = KS * D * D
    enc_weight = shared[:enc_size].reshape(KS * HOP, D)
    dec_weight = shared[enc_size:enc_size + dec_size].reshape(KS * D, D)
    out_weight = shared[enc_size + dec_size:].reshape(D, HOP)
    return (enc_weight, dec_weight, out_weight)

def pick_codes(codebook, block_codes, group_idx, clip_count):
    picked = jnp.zeros((clip_count, SLOT, GD), jnp.float32)
    for level_idx in range(LEVELS):
        picked = picked + jnp.take(codebook[group_idx, level_idx], block_codes[:, group_idx, level_idx], axis=0)
    return picked

def make_gap(shared, table, signal, block_codes):
    enc_weight = split_weights(shared)[0]
    codebook = table.reshape(GROUPS, LEVELS, CB, GD)
    z_sent = high_dot(stack_three(signal), enc_weight).astype(jnp.bfloat16).astype(jnp.float32)
    pieces = [pick_codes(codebook, block_codes, group_idx, signal.shape[0]) for group_idx in range(GROUPS)]
    return jnp.concatenate(pieces, axis=2) - z_sent

def block_loss(shared, table, disc_weight, disc_score, spec_tab, signal, masks, block_codes, gap):
    enc_weight, dec_weight, out_weight = split_weights(shared)
    codebook = table.reshape(GROUPS, LEVELS, CB, GD)
    mask_three = masks[..., None]
    encoded = high_dot(stack_three(signal), enc_weight)
    z_sent = low_back(low(encoded))
    commit = jnp.float32(0.0)
    for group_idx in range(GROUPS):
        picked = low_back(pick_codes(codebook, block_codes, group_idx, signal.shape[0]))
        z_part = z_sent[..., group_idx * GD:(group_idx + 1) * GD]
        commit = commit + jnp.sum(mask_three * (z_part - picked) ** 2)
    quant = (z_sent + gap) * mask_three
    q_sent = low_back(low(quant))
    pre_dec = low_back(high_dot(stack_three(q_sent), dec_weight))
    hidden = low(jax.nn.silu(pre_dec))
    pre_out = low_back(high_dot(hidden, out_weight))
    made = jnp.tanh(pre_out) * mask_three
    recon = jnp.sum(mask_three * smooth_cost(made - signal)) / HOP
    made_low = low(made)
    spec_fake = low_back(high_dot(made_low, spec_tab))
    spec_real = high_dot(signal, spec_tab)
    spectral = jnp.sum(mask_three * smooth_cost(magnitude(spec_fake) - magnitude(spec_real))) / HOP
    feat_fake = jax.nn.silu(low_back(high_dot(stack_three(made_low), disc_weight)))
    feat_real = jax.nn.silu(high_dot(stack_three(signal), disc_weight))
    score = lax.optimization_barrier(jnp.sum(feat_fake * disc_score, axis=2))
    adverse = jnp.sum(masks * (1.0 - score) ** 2)
    feature = jnp.sum(mask_three * smooth_cost(feat_fake - feat_real)) / D
    return recon + spectral + adverse + feature + commit / D

def reference(audio, lengths, codes, disc_weight, disc_score, params, params_mom, params_avg, books, books_mom, books_avg):
    masks = (jnp.arange(SLOT)[None, :] < lengths[:, None]).astype(jnp.float32)
    signal = audio.astype(jnp.float32) * masks[..., None]
    blocks = CLIPS // 16
    block_data = (signal.reshape(blocks, 16, SLOT, HOP), masks.reshape(blocks, 16, SLOT), jnp.transpose(codes, (2, 0, 1, 3)).reshape(blocks, 16, GROUPS, LEVELS, SLOT))
    disc_float = disc_weight.astype(jnp.float32)
    spec_tab = spectral_table(HOP).astype(jnp.bfloat16).astype(jnp.float32)
    fixed_shared = params.astype(jnp.bfloat16).astype(jnp.float32)
    fixed_table = books.astype(jnp.bfloat16).astype(jnp.float32)
    gaps = lax.map(lambda piece: make_gap(fixed_shared, fixed_table, piece[0], piece[2]), block_data)

    def total(shared_in, table_in):
        shared = low(shared_in)
        table = low(table_in)
        checked = jax.checkpoint(block_loss)

        def scan_step(running, piece):
            return (running + checked(shared, table, disc_float, disc_score, spec_tab, piece[0], piece[1], piece[2], piece[3]), None)
        result, unused = lax.scan(scan_step, jnp.zeros((), jnp.float32), block_data + (gaps,))
        return result
    loss_sum, pull = jax.vjp(total, params, books)
    grad_shared, grad_table = pull(jnp.ones((), loss_sum.dtype))
    frame_count = jnp.sum(masks)
    grad_shared = grad_shared / frame_count
    grad_table = grad_table / frame_count
    root = math.sqrt(131.0 * CLIPS)
    spots = jnp.arange(P_SIZE)
    rate = jnp.where(spots < KS * HOP * D, 0.65, jnp.where(spots < KS * HOP * D + KS * D * D, 0.14, 0.2)) * root
    mom_new = MOMENTUM * params_mom + grad_shared
    param_new = params - rate * (grad_shared + MOMENTUM * mom_new)
    avg_new = AVERAGE * params_avg + (1.0 - AVERAGE) * param_new
    book_rate = 3.9 * math.sqrt(131.0 * CLIPS * CB)
    book_mom_new = MOMENTUM * books_mom + grad_table
    book_new = books - book_rate * (grad_table + MOMENTUM * book_mom_new)
    book_avg_new = AVERAGE * books_avg + (1.0 - AVERAGE) * book_new
    return (param_new, mom_new, avg_new, book_new, book_mom_new, book_avg_new, loss_sum, frame_count)
```

```python
import math

import jax
import jax.numpy as jnp
import numpy as np
from jax import lax
from jax.experimental import pallas as pl
from jax.experimental.pallas import tpu as pltpu
from jax.sharding import PartitionSpec as P

BF = jnp.bfloat16
F32 = jnp.float32
MOMENTUM = 0.9
AVERAGE = 0.99
LANES = 256
CB = 1024
WIDE = 512


def spectral_table(samples):
    spots = np.arange(samples)[:, None]
    bins = np.arange(samples // 2)[None, :]
    turns = (spots * bins % samples) * (2.0 * math.pi / samples)
    window = 0.5 - 0.5 * np.cos((spots + 0.5) * (2.0 * math.pi / samples))
    table = np.concatenate([window * np.cos(turns), window * np.sin(turns)], axis=1)
    return (table * math.sqrt(2.0 / samples)).astype(np.float32)


def dot(left, right):
    return jnp.dot(left, right, preferred_element_type=F32)


def dot_nt(left, right):
    return lax.dot_general(left, right, (((1,), (1,)), ((), ())), preferred_element_type=F32)


def lanes(index, width):
    return pl.ds(pl.multiple_of(index * width, width), width)


def col_sum(values):
    return jnp.sum(values, axis=0, keepdims=True)


def before(values):
    return pltpu.roll(values, 1, 1)


def after(values):
    return pltpu.roll(values, values.shape[1] - 1, 1)


def stack_three(values):
    return jnp.concatenate([before(values), values, after(values)], axis=0)


def silu_parts(values):
    sigmoid = 0.5 * jnp.tanh(0.5 * values) + 0.5
    return values * sigmoid, sigmoid * (1.0 + values * (1.0 - sigmoid))


def silu(values):
    return values * (0.5 * jnp.tanh(0.5 * values) + 0.5)


def load_signal(clip_count, side, aud, lens, codes, pad, ipad, crow, mask, sig):
    slots = aud.shape[2]
    samples = aud.shape[1]
    pad[...] = jnp.zeros_like(pad)
    ipad[...] = jnp.full(ipad.shape, -1, jnp.int32)
    spots = lax.broadcasted_iota(jnp.int32, (1, LANES), 1)

    def step(clip, carry):
        here = lanes(clip, LANES)
        row = side * clip_count + clip
        own = (spots < lens[row]).astype(F32)
        mask[:, here] = own
        for which in range(4):
            ipad[which : which + 1, 0:slots] = codes[which // 2, which % 2, pl.ds(row, 1), :]
        crow[:, here] = ipad[...]
        pad[:, 0:slots] = aud[clip]
        wave = pad[...].astype(F32) * own
        sig[:, here] = wave.astype(BF)
        return carry

    lax.fori_loop(0, clip_count, step, 0)


def real_side(clip_count, sig, disc_t, spec_t, feat_real, mag_real):
    samples = spec_t.shape[0]
    half = samples // 2

    def step(pair, carry):
        here = lanes(pair, WIDE)
        wave = sig[:, here]
        feat_real[:, here] = silu(dot(disc_t[...], stack_three(wave))).astype(BF)
        spec = dot(spec_t[...], wave)
        norm = spec[:half] * spec[:half] + spec[half:] * spec[half:] + 1.0
        mag_real[:, here] = jnp.sqrt(norm)
        return carry

    lax.fori_loop(0, clip_count * LANES // WIDE, step, 0)


def onehot(crow, which, here, count):
    entries = lax.broadcasted_iota(jnp.int32, (CB, count), 0)
    return (entries == crow[pl.ds(which, 1), here]).astype(F32).astype(BF)


def pick(clip_count, crow, mask, books_t, quant, low):
    half = books_t.shape[1]

    def step(pair, carry):
        here = lanes(pair, WIDE)
        own = mask[:, here]
        for group in range(2):
            hot = jnp.concatenate(
                [onehot(crow, 2 * group, here, WIDE), onehot(crow, 2 * group + 1, here, WIDE)], 0
            )
            value = dot(books_t[group], hot) * own
            high = value.astype(BF)
            spot = group * half
            low[spot : spot + half, here] = (value - high.astype(F32)).astype(BF)
            quant[spot : spot + half, here] = high
        return carry

    lax.fori_loop(0, clip_count * LANES // WIDE, step, 0)


def encode(clip_count, enc_t, sig, quant, low, mask, slope, loss):
    width = enc_t.shape[0]

    def step(pair, carry):
        here = lanes(pair, WIDE)
        latent = dot(enc_t[...], stack_three(sig[:, here])).astype(BF).astype(F32)
        value = quant[:, here].astype(F32) + low[:, here].astype(F32)
        gap = (latent - value) * mask[:, here]
        loss[...] += col_sum(gap * gap) * (1.0 / width)
        slope[:, here] = (gap * (-2.0 / width)).astype(BF)
        return carry

    lax.fori_loop(0, clip_count * LANES // WIDE, step, 0)


def book_grad(clip_count, crow, slope, which, group_rows):
    total = None
    chunk = 4 * LANES
    for part in range(clip_count * LANES // chunk):
        here = pl.ds(part * chunk, chunk)
        term = dot_nt(onehot(crow, which, here, chunk), slope[group_rows, here])
        total = term if total is None else total + term
    return total


def decode(clip_count, refs, loss):
    (quant, dec_t, out, out_t, mask, sig, spec, spec_t, disc, disc_t, score_col) = refs[:11]
    (feat_real, mag_real, hidden, d_out, d_dec) = refs[11:]
    samples = spec.shape[0]
    width = hidden.shape[0]
    half = samples // 2

    def step(pair, carry):
        here = lanes(pair, WIDE)
        own = mask[:, here]
        pre_dec = dot(dec_t[...], stack_three(quant[:, here]))
        act, act_slope = silu_parts(pre_dec)
        act = act.astype(BF)
        hidden[:, here] = act
        tanh_out = jnp.tanh(dot(out_t[...], act))
        made = tanh_out * own
        wave_gap = made - sig[:, here].astype(F32)
        norm = wave_gap * wave_gap + 1.0
        root = lax.rsqrt(norm)
        lost = col_sum(norm * root - 1.0) * (1.0 / samples)
        d_made = wave_gap * root * (1.0 / samples)
        made_low = made.astype(BF)

        spec_fake = dot(spec_t[...], made_low)
        real_part, imag_part = spec_fake[:half], spec_fake[half:]
        norm = real_part * real_part + imag_part * imag_part + 1.0
        root = lax.rsqrt(norm)
        spec_gap = norm * root - mag_real[:, here]
        norm = spec_gap * spec_gap + 1.0
        gap_root = lax.rsqrt(norm)
        lost += col_sum(norm * gap_root - 1.0) * (1.0 / samples)
        d_mag = spec_gap * gap_root * root * (1.0 / samples)
        d_spec = jnp.concatenate([d_mag * real_part, d_mag * imag_part], axis=0).astype(BF)
        d_made += dot(spec[...], d_spec)

        pre_fake = dot(disc_t[...], stack_three(made_low))
        feat_fake, feat_slope = silu_parts(pre_fake)
        weight = jnp.concatenate([score_col[...]] * (WIDE // 128), axis=1)
        miss = 1.0 - col_sum(feat_fake * weight)
        feat_gap = feat_fake - feat_real[:, here].astype(F32)
        norm = feat_gap * feat_gap + 1.0
        root = lax.rsqrt(norm)
        lost += own * (miss * miss + col_sum(norm * root - 1.0) * (1.0 / width))
        d_feat = (-2.0 * own * miss) * weight + (own * (1.0 / width)) * (feat_gap * root)
        d_fake = (d_feat * feat_slope).astype(BF)
        back = dot(disc[...], d_fake)
        d_made += after(back[:samples]) + back[samples : 2 * samples] + before(back[2 * samples :])

        d_pre_out = (d_made * own * (1.0 - tanh_out * tanh_out)).astype(BF)
        d_out[:, here] = d_pre_out
        d_dec[:, here] = (dot(out[...], d_pre_out) * act_slope).astype(BF)
        loss[...] += lost
        return carry

    lax.fori_loop(0, clip_count * LANES // WIDE, step, 0)


def latent_back(clip_count, dec, d_dec, mask, slope, d_latent):
    width = d_dec.shape[0]

    def step(pair, carry):
        here = lanes(pair, WIDE)
        back = dot(dec[...], d_dec[:, here])
        joined = after(back[:width]) + back[width : 2 * width] + before(back[2 * width :])
        joined = joined.astype(BF).astype(F32) * mask[:, here]
        d_latent[:, here] = (joined - slope[:, here].astype(F32)).astype(BF)
        return carry

    lax.fori_loop(0, clip_count * LANES // WIDE, step, 0)


def local_kernel(
    aud, lens, codes, disc, score, spec, spec_t, enc, dec, out, books,
    g_enc, g_dec, g_out, g_books, loss_out,
    pad, ipad, crow, mask, sig, disc_t, score_col, feat_real, mag_real,
    books_t, quant, hidden, enc_t, slope, dec_t, out_t, d_out, d_dec, loss,
    met, send_sem, recv_sem,
):
    clip_count = aud.shape[0]
    side = lax.axis_index("grp")
    spot = lax.axis_index("dp")
    barrier = pltpu.get_barrier_semaphore()
    pl.semaphore_signal(
        barrier, inc=1, device_id=(spot, 1 - side), device_id_type=pl.DeviceIdType.MESH
    )
    pl.semaphore_wait(barrier, 1)
    loss[...] = jnp.zeros_like(loss)
    disc_t[...] = jnp.transpose(disc[...])
    score_col[...] = jnp.transpose(jnp.broadcast_to(score[...], (128, score.shape[1])))
    load_signal(clip_count, side, aud, lens, codes, pad, ipad, crow, mask, sig)
    real_side(clip_count, sig, disc_t, spec_t, feat_real, mag_real)
    for group in range(2):
        books_t[group] = jnp.transpose(books[group])
    pick(clip_count, crow, mask, books_t, quant, hidden)
    enc_t[...] = jnp.transpose(enc[...])
    dec_t[...] = jnp.transpose(dec[...])
    out_t[...] = jnp.transpose(out[...])
    encode(clip_count, enc_t, sig, quant, hidden, mask, slope, loss)

    def book_step(which, carry):
        rows = pl.ds(pl.multiple_of(which // 2 * 256, 256), 256)
        g_books[which] = book_grad(clip_count, crow, slope, which, rows)
        return carry

    lax.fori_loop(0, 4, book_step, 0)
    decode(
        clip_count,
        (quant, dec_t, out, out_t, mask, sig, spec, spec_t, disc, disc_t, score_col,
         feat_real, mag_real, hidden, d_out, d_dec),
        loss,
    )
    g_out[...] = dot_nt(hidden[...], d_out[...])

    width = quant.shape[0]
    for part, shift in enumerate((before, lambda values: values, after)):
        g_dec[part * width : (part + 1) * width, :] = dot_nt(shift(quant[...]), d_dec[...])
    latent_back(clip_count, dec, d_dec, mask, slope, hidden)

    samples = sig.shape[0]
    for part, shift in enumerate((before, lambda values: values, after)):
        g_enc[part * samples : (part + 1) * samples, :] = dot_nt(shift(sig[...]), hidden[...])
    swap = pltpu.make_async_remote_copy(
        src_ref=loss, dst_ref=met, send_sem=send_sem, recv_sem=recv_sem,
        device_id=(spot, 1 - side), device_id_type=pl.DeviceIdType.MESH,
    )
    swap.start()
    swap.wait()
    loss_out[...] = loss[...] + met[...]


def local_call(audio_t, lengths, codes, disc, score, enc, dec, out, books):
    clip_count, samples, _ = audio_t.shape
    width = disc.shape[1]
    total = clip_count * LANES
    table = spectral_table(samples)
    vmem = pl.BlockSpec(memory_space=pltpu.VMEM)
    smem = pl.BlockSpec(memory_space=pltpu.SMEM)
    return pl.pallas_call(
        local_kernel,
        out_shape=(
            jax.ShapeDtypeStruct((3 * samples, width), F32),
            jax.ShapeDtypeStruct((3 * width, width), F32),
            jax.ShapeDtypeStruct((width, samples), F32),
            jax.ShapeDtypeStruct((4, CB, width // 2), F32),
            jax.ShapeDtypeStruct((1, WIDE), F32),
        ),
        in_specs=[vmem, smem] + [vmem] * 9,
        out_specs=[vmem] * 5,
        scratch_shapes=[
            pltpu.VMEM((samples, LANES), BF),
            pltpu.VMEM((8, LANES), jnp.int32),
            pltpu.VMEM((8, total), jnp.int32),
            pltpu.VMEM((1, total), F32),
            pltpu.VMEM((samples, total), BF),
            pltpu.VMEM((width, 3 * samples), BF),
            pltpu.VMEM((width, 128), F32),
            pltpu.VMEM((width, total), BF),
            pltpu.VMEM((samples // 2, total), F32),
            pltpu.VMEM((2, width // 2, 2 * CB), BF),
            pltpu.VMEM((width, total), BF),
            pltpu.VMEM((width, total), BF),
            pltpu.VMEM((width, 3 * samples), BF),
            pltpu.VMEM((width, total), BF),
            pltpu.VMEM((width, 3 * width), BF),
            pltpu.VMEM((samples, width), BF),
            pltpu.VMEM((samples, total), BF),
            pltpu.VMEM((width, total), BF),
            pltpu.VMEM((1, WIDE), F32),
            pltpu.VMEM((1, WIDE), F32),
            pltpu.SemaphoreType.DMA,
            pltpu.SemaphoreType.DMA,
        ],
        compiler_params=pltpu.CompilerParams(
            vmem_limit_bytes=56 << 20, collective_id=0, has_side_effects=True
        ),
        name="train_local",
    )(
        audio_t, lengths, codes, disc, score.reshape(1, width),
        jnp.asarray(table, BF), jnp.asarray(table.T, BF), enc, dec, out, books,
    )


def shards(
    audio, lengths, codes, disc_weight, disc_score, params, params_mom, params_avg, books,
    books_mom, books_avg,
):
    clip_count, slot_count, samples = audio.shape
    width = disc_weight.shape[1]
    half_width = width // 2
    side = lax.axis_index("grp")
    shared = lax.all_gather(params.astype(BF), "dp", axis=0, tiled=True)
    table = lax.all_gather(books.astype(BF), ("grp", "dp"), axis=1, tiled=True)
    enc_size = 3 * samples * width
    dec_size = 3 * width * width
    enc_weight = shared[:enc_size].reshape(3 * samples, width)
    dec_weight = shared[enc_size : enc_size + dec_size].reshape(3 * width, width)
    out_weight = shared[enc_size + dec_size :].reshape(width, samples)
    codebook = table.reshape(2, 2 * CB, half_width)
    local_count = jnp.sum(
        lax.dynamic_slice_in_dim(lengths, side * clip_count, clip_count, 0)
    ).astype(F32)
    frame_count = lax.psum(local_count, ("dp", "grp"))
    grad_enc, grad_dec, grad_out, grad_book, lost = local_call(
        jnp.swapaxes(audio, 1, 2), lengths, codes, disc_weight, disc_score,
        enc_weight, dec_weight, out_weight, codebook,
    )
    grad_shared = jnp.concatenate(
        [grad_enc.reshape(-1), grad_dec.reshape(-1), grad_out.reshape(-1)]
    )
    grad_shared = lax.psum(grad_shared.astype(BF), "grp").astype(F32)
    grad_book = lax.psum_scatter(
        grad_book.reshape(2, -1), "grp", scatter_dimension=0, tiled=True
    )
    shared_part = lax.psum_scatter(grad_shared, "dp", scatter_dimension=0, tiled=True)
    book_part = lax.psum_scatter(grad_book, "dp", scatter_dimension=1, tiled=True)
    loss_sum = lax.psum(jnp.sum(lost), "dp")
    all_clips = clip_count * lax.axis_size("dp") * lax.axis_size("grp")
    root = math.sqrt(131.0 * all_clips)
    shard_length = params.shape[0]
    spots = lax.axis_index("dp") * shard_length + jnp.arange(shard_length)
    rate = (
        jnp.where(spots < enc_size, 0.65, jnp.where(spots < enc_size + dec_size, 0.14, 0.2)) * root
    )
    shared_grad = shared_part / frame_count
    mom_new = MOMENTUM * params_mom + shared_grad
    param_new = params - rate * (shared_grad + MOMENTUM * mom_new)
    avg_new = AVERAGE * params_avg + (1.0 - AVERAGE) * param_new
    book_rate = 3.9 * math.sqrt(131.0 * all_clips * CB)
    book_grad_mean = book_part / frame_count
    book_mom_new = MOMENTUM * books_mom + book_grad_mean
    book_new = books - book_rate * (book_grad_mean + MOMENTUM * book_mom_new)
    book_avg_new = AVERAGE * books_avg + (1.0 - AVERAGE) * book_new
    return (
        param_new, mom_new, avg_new, book_new, book_mom_new, book_avg_new, loss_sum, frame_count,
    )


def solution(mesh):
    in_specs = (
        P(("dp", "grp"), None, None), P("dp"), P(None, None, "dp", None), P(), P(), P("dp"),
        P("dp"), P("dp"), P("grp", "dp"), P("grp", "dp"), P("grp", "dp"),
    )
    out_specs = (
        P("dp"), P("dp"), P("dp"), P("grp", "dp"), P("grp", "dp"), P("grp", "dp"), P(), P(),
    )
    return jax.shard_map(shards, mesh=mesh, in_specs=in_specs, out_specs=out_specs, check_vma=False)
```

```python
import functools
import math

import jax
import jax.numpy as jnp
import numpy as np
from jax import lax
from jax.experimental import pallas as pl
from jax.experimental.pallas import tpu as pltpu
from jax.sharding import PartitionSpec as P

BF = jnp.bfloat16
F32 = jnp.float32
MOMENTUM = 0.9
AVERAGE = 0.99
LANES = 256
CB = 1024
WIDE = 512
VMEM_LIMIT = 56 << 20


def spectral_table(samples):
    spots = np.arange(samples)[:, None]
    bins = np.arange(samples // 2)[None, :]
    turns = (spots * bins % samples) * (2.0 * math.pi / samples)
    window = 0.5 - 0.5 * np.cos((spots + 0.5) * (2.0 * math.pi / samples))
    table = np.concatenate([window * np.cos(turns), window * np.sin(turns)], axis=1)
    return (table * math.sqrt(2.0 / samples)).astype(np.float32)


def dot(left, right):
    return jnp.dot(left, right, preferred_element_type=F32)


def dot_nt(left, right):
    return lax.dot_general(left, right, (((1,), (1,)), ((), ())), preferred_element_type=F32)


def lanes(index, width):
    return pl.ds(pl.multiple_of(index * width, width), width)


def col_sum(values):
    return jnp.sum(values, axis=0, keepdims=True)


def before(values):
    return pltpu.roll(values, 1, 1)


def after(values):
    return pltpu.roll(values, values.shape[1] - 1, 1)


def stack_three(values):
    return jnp.concatenate([before(values), values, after(values)], axis=0)


def silu_parts(values):
    sigmoid = 0.5 * jnp.tanh(0.5 * values) + 0.5
    return values * sigmoid, sigmoid * (1.0 + values * (1.0 - sigmoid))


def silu(values):
    return values * (0.5 * jnp.tanh(0.5 * values) + 0.5)


def load_signal(clip_count, side, fetch, free, lens, codes, pad, ipad, crow, mask, sig):
    slots = codes.shape[3]
    pad[...] = jnp.zeros_like(pad)
    ipad[...] = jnp.full(ipad.shape, -1, jnp.int32)
    spots = lax.broadcasted_iota(jnp.int32, (1, LANES), 1)

    def step(clip, carry):
        here = lanes(clip, LANES)
        row = side * clip_count + clip
        own = (spots < lens[row]).astype(F32)
        mask[:, here] = own
        for which in range(4):
            ipad[which : which + 1, 0:slots] = codes[which // 2, which % 2, pl.ds(row, 1), :]
        crow[:, here] = ipad[...]
        pad[:, 0:slots] = fetch(clip)[...]
        free(clip)
        wave = pad[...].astype(F32) * own
        sig[:, here] = wave.astype(BF)
        return carry

    lax.fori_loop(0, clip_count, step, 0)


def real_side(pairs, sig, disc_t, spec_t, feat_real, mag_real):
    samples = spec_t.shape[0]
    half = samples // 2

    def step(pair, carry):
        here = lanes(pair, WIDE)
        wave = sig[:, here]
        feat_real[:, here] = silu(dot(disc_t[...], stack_three(wave))).astype(BF)
        spec = dot(spec_t[...], wave)
        norm = spec[:half] * spec[:half] + spec[half:] * spec[half:] + 1.0
        mag_real[:, here] = jnp.sqrt(norm)
        return carry

    lax.fori_loop(*pairs, step, 0)


def onehot(crow, which, here, count):
    entries = lax.broadcasted_iota(jnp.int32, (CB, count), 0)
    return (entries == crow[pl.ds(which, 1), here]).astype(F32).astype(BF)


def pick(pairs, crow, mask, books_t, quant, low):
    half = books_t.shape[1]

    def step(pair, carry):
        here = lanes(pair, WIDE)
        own = mask[:, here]
        for group in range(2):
            hot = jnp.concatenate(
                [onehot(crow, 2 * group, here, WIDE), onehot(crow, 2 * group + 1, here, WIDE)], 0
            )
            value = dot(books_t[group], hot) * own
            high = value.astype(BF)
            spot = group * half
            low[spot : spot + half, here] = (value - high.astype(F32)).astype(BF)
            quant[spot : spot + half, here] = high
        return carry

    lax.fori_loop(*pairs, step, 0)


def encode(pairs, enc_t, sig, quant, low, mask, slope, loss):
    width = enc_t.shape[0]

    def step(pair, carry):
        here = lanes(pair, WIDE)
        latent = dot(enc_t[...], stack_three(sig[:, here])).astype(BF).astype(F32)
        value = quant[:, here].astype(F32) + low[:, here].astype(F32)
        gap = (latent - value) * mask[:, here]
        loss[...] += col_sum(gap * gap) * (1.0 / width)
        slope[:, here] = (gap * (-2.0 / width)).astype(BF)
        return carry

    lax.fori_loop(*pairs, step, 0)


def book_grad(clip_count, crow, slope, which, rows):
    total = None
    chunk = 4 * LANES
    for part in range(clip_count * LANES // chunk):
        here = pl.ds(part * chunk, chunk)
        term = dot_nt(onehot(crow, which, here, chunk), slope[rows, here])
        total = term if total is None else total + term
    return total


def decode(pairs, refs, loss):
    (quant, dec_t, out, out_t, mask, sig, spec, spec_t, disc, disc_t, score_col) = refs[:11]
    (feat_real, mag_real, hidden, d_out, d_dec) = refs[11:]
    samples = spec.shape[0]
    width = hidden.shape[0]
    half = samples // 2

    def step(pair, carry):
        here = lanes(pair, WIDE)
        own = mask[:, here]
        pre_dec = dot(dec_t[...], stack_three(quant[:, here]))
        act, act_slope = silu_parts(pre_dec)
        act = act.astype(BF)
        hidden[:, here] = act
        tanh_out = jnp.tanh(dot(out_t[...], act))
        made = tanh_out * own
        wave_gap = made - sig[:, here].astype(F32)
        norm = wave_gap * wave_gap + 1.0
        root = lax.rsqrt(norm)
        lost = col_sum(norm * root - 1.0) * (1.0 / samples)
        d_made = wave_gap * root * (1.0 / samples)
        made_low = made.astype(BF)

        spec_fake = dot(spec_t[...], made_low)
        real_part, imag_part = spec_fake[:half], spec_fake[half:]
        norm = real_part * real_part + imag_part * imag_part + 1.0
        root = lax.rsqrt(norm)
        spec_gap = norm * root - mag_real[:, here]
        norm = spec_gap * spec_gap + 1.0
        gap_root = lax.rsqrt(norm)
        lost += col_sum(norm * gap_root - 1.0) * (1.0 / samples)
        d_mag = spec_gap * gap_root * root * (1.0 / samples)
        d_spec = jnp.concatenate([d_mag * real_part, d_mag * imag_part], axis=0).astype(BF)
        d_made += dot(spec[...], d_spec)

        pre_fake = dot(disc_t[...], stack_three(made_low))
        feat_fake, feat_slope = silu_parts(pre_fake)
        weight = jnp.concatenate([score_col[...]] * (WIDE // 128), axis=1)
        miss = 1.0 - col_sum(feat_fake * weight)
        feat_gap = feat_fake - feat_real[:, here].astype(F32)
        norm = feat_gap * feat_gap + 1.0
        root = lax.rsqrt(norm)
        lost += own * (miss * miss + col_sum(norm * root - 1.0) * (1.0 / width))
        d_feat = (-2.0 * own * miss) * weight + (own * (1.0 / width)) * (feat_gap * root)
        d_fake = (d_feat * feat_slope).astype(BF)
        back = dot(disc[...], d_fake)
        d_made += after(back[:samples]) + back[samples : 2 * samples] + before(back[2 * samples :])

        d_pre_out = (d_made * own * (1.0 - tanh_out * tanh_out)).astype(BF)
        d_out[:, here] = d_pre_out
        d_dec[:, here] = (dot(out[...], d_pre_out) * act_slope).astype(BF)
        loss[...] += lost
        return carry

    lax.fori_loop(*pairs, step, 0)


def latent_back(pairs, dec, d_dec, mask, slope, d_latent):
    width = d_dec.shape[0]

    def step(pair, carry):
        here = lanes(pair, WIDE)
        back = dot(dec[...], d_dec[:, here])
        joined = after(back[:width]) + back[width : 2 * width] + before(back[2 * width :])
        joined = joined.astype(BF).astype(F32) * mask[:, here]
        d_latent[:, here] = (joined - slope[:, here].astype(F32)).astype(BF)
        return carry

    lax.fori_loop(*pairs, step, 0)


def local_kernel(
    aud, lens, codes, disc, score, spec, spec_t, enc, dec, out, books,
    g_enc, g_dec, g_out, g_books, loss_out,
    pad, ipad, crow, mask, sig, disc_t, score_col, feat_real, mag_real,
    books_t, quant, hidden, enc_t, slope, dec_t, out_t, d_out, d_dec, loss,
):
    clip_count = aud.shape[0]
    pairs = (0, clip_count * LANES // WIDE)
    side = lax.axis_index("grp")
    loss[...] = jnp.zeros_like(loss)
    disc_t[...] = jnp.transpose(disc[...])
    score_col[...] = jnp.transpose(jnp.broadcast_to(score[...], (128, score.shape[1])))
    load_signal(
        clip_count, side, lambda clip: aud.at[clip], lambda clip: None, lens, codes, pad, ipad,
        crow, mask, sig,
    )
    real_side(pairs, sig, disc_t, spec_t, feat_real, mag_real)
    for group in range(2):
        books_t[group] = jnp.transpose(books[group])
    pick(pairs, crow, mask, books_t, quant, hidden)
    enc_t[...] = jnp.transpose(enc[...])
    dec_t[...] = jnp.transpose(dec[...])
    out_t[...] = jnp.transpose(out[...])
    encode(pairs, enc_t, sig, quant, hidden, mask, slope, loss)

    def book_step(which, carry):
        rows = pl.ds(pl.multiple_of(which // 2 * 256, 256), 256)
        g_books[which] = book_grad(clip_count, crow, slope, which, rows)
        return carry

    lax.fori_loop(0, 4, book_step, 0)
    decode(
        pairs,
        (quant, dec_t, out, out_t, mask, sig, spec, spec_t, disc, disc_t, score_col,
         feat_real, mag_real, hidden, d_out, d_dec),
        loss,
    )
    g_out[...] = dot_nt(hidden[...], d_out[...])

    width = quant.shape[0]
    for part, shift in enumerate((before, lambda values: values, after)):
        g_dec[part * width : (part + 1) * width, :] = dot_nt(shift(quant[...]), d_dec[...])
    latent_back(pairs, dec, d_dec, mask, slope, hidden)

    samples = sig.shape[0]
    for part, shift in enumerate((before, lambda values: values, after)):
        g_enc[part * samples : (part + 1) * samples, :] = dot_nt(shift(sig[...]), hidden[...])
    loss_out[...] = loss[...]


def local_call(audio_t, lengths, codes, disc, score, enc, dec, out, books):
    clip_count, samples, _ = audio_t.shape
    width = disc.shape[1]
    total = clip_count * LANES
    table = spectral_table(samples)
    vmem = pl.BlockSpec(memory_space=pltpu.VMEM)
    smem = pl.BlockSpec(memory_space=pltpu.SMEM)
    return pl.pallas_call(
        local_kernel,
        out_shape=(
            jax.ShapeDtypeStruct((3 * samples, width), F32),
            jax.ShapeDtypeStruct((3 * width, width), F32),
            jax.ShapeDtypeStruct((width, samples), F32),
            jax.ShapeDtypeStruct((4, CB, width // 2), F32),
            jax.ShapeDtypeStruct((1, WIDE), F32),
        ),
        in_specs=[vmem, smem] + [vmem] * 9,
        out_specs=[vmem] * 5,
        scratch_shapes=[
            pltpu.VMEM((samples, LANES), BF),
            pltpu.VMEM((8, LANES), jnp.int32),
            pltpu.VMEM((8, total), jnp.int32),
            pltpu.VMEM((1, total), F32),
            pltpu.VMEM((samples, total), BF),
            pltpu.VMEM((width, 3 * samples), BF),
            pltpu.VMEM((width, 128), F32),
            pltpu.VMEM((width, total), BF),
            pltpu.VMEM((samples // 2, total), F32),
            pltpu.VMEM((2, width // 2, 2 * CB), BF),
            pltpu.VMEM((width, total), BF),
            pltpu.VMEM((width, total), BF),
            pltpu.VMEM((width, 3 * samples), BF),
            pltpu.VMEM((width, total), BF),
            pltpu.VMEM((width, 3 * width), BF),
            pltpu.VMEM((samples, width), BF),
            pltpu.VMEM((samples, total), BF),
            pltpu.VMEM((width, total), BF),
            pltpu.VMEM((1, WIDE), F32),
        ],
        compiler_params=pltpu.CompilerParams(vmem_limit_bytes=56 << 20),
        name="train_local",
    )(
        audio_t, lengths, codes, disc, score.reshape(1, width),
        jnp.asarray(table, BF), jnp.asarray(table.T, BF), enc, dec, out, books,
    )


def shards(
    audio, lengths, codes, disc_weight, disc_score, params, params_mom, params_avg, books,
    books_mom, books_avg,
):
    clip_count, slot_count, samples = audio.shape
    width = disc_weight.shape[1]
    half_width = width // 2
    side = lax.axis_index("grp")
    shared = lax.all_gather(params.astype(BF), "dp", axis=0, tiled=True)
    table = lax.all_gather(books.astype(BF), ("grp", "dp"), axis=1, tiled=True)
    enc_size = 3 * samples * width
    dec_size = 3 * width * width
    enc_weight = shared[:enc_size].reshape(3 * samples, width)
    dec_weight = shared[enc_size : enc_size + dec_size].reshape(3 * width, width)
    out_weight = shared[enc_size + dec_size :].reshape(width, samples)
    codebook = table.reshape(2, 2 * CB, half_width)
    local_count = jnp.sum(
        lax.dynamic_slice_in_dim(lengths, side * clip_count, clip_count, 0)
    ).astype(F32)
    frame_count = lax.psum(local_count, ("dp", "grp"))
    grad_enc, grad_dec, grad_out, grad_book, lost = local_call(
        jnp.swapaxes(audio, 1, 2), lengths, codes, disc_weight, disc_score,
        enc_weight, dec_weight, out_weight, codebook,
    )
    grad_shared = jnp.concatenate(
        [grad_enc.reshape(-1), grad_dec.reshape(-1), grad_out.reshape(-1)]
    )
    grad_shared = lax.psum(grad_shared.astype(BF), "grp").astype(F32)
    grad_book = lax.psum_scatter(
        grad_book.reshape(2, -1), "grp", scatter_dimension=0, tiled=True
    )
    shared_part = lax.psum_scatter(grad_shared, "dp", scatter_dimension=0, tiled=True)
    book_part = lax.psum_scatter(grad_book, "dp", scatter_dimension=1, tiled=True)
    loss_sum = lax.psum(jnp.sum(lost), ("dp", "grp"))
    all_clips = clip_count * lax.axis_size("dp") * lax.axis_size("grp")
    root = math.sqrt(131.0 * all_clips)
    shard_length = params.shape[0]
    spots = lax.axis_index("dp") * shard_length + jnp.arange(shard_length)
    rate = (
        jnp.where(spots < enc_size, 0.65, jnp.where(spots < enc_size + dec_size, 0.14, 0.2)) * root
    )
    shared_grad = shared_part / frame_count
    mom_new = MOMENTUM * params_mom + shared_grad
    param_new = params - rate * (shared_grad + MOMENTUM * mom_new)
    avg_new = AVERAGE * params_avg + (1.0 - AVERAGE) * param_new
    book_rate = 3.9 * math.sqrt(131.0 * all_clips * CB)
    book_grad_mean = book_part / frame_count
    book_mom_new = MOMENTUM * books_mom + book_grad_mean
    book_new = books - book_rate * (book_grad_mean + MOMENTUM * book_mom_new)
    book_avg_new = AVERAGE * books_avg + (1.0 - AVERAGE) * book_new
    return (
        param_new, mom_new, avg_new, book_new, book_mom_new, book_avg_new, loss_sum, frame_count,
    )


MESH = pl.DeviceIdType.MESH
ENC_RATE, DEC_RATE, OUT_RATE, BOOK_RATE = 0.65, 0.14, 0.2, 3.9
CHIPS = (4, 2, 2)
COPIES = 80
WAVES = 4


def cols(index, width=128):
    return slice(index * width, (index + 1) * width)


def unflatten_out(flat, square):
    count = square.shape[1] // 2
    left = lax.broadcasted_iota(jnp.int32, (count, 128), 1) < 64
    part = [flat[pl.ds(k, count, stride=5), :] for k in range(5)]
    turned = [pltpu.roll(part[k], 64, 1) for k in (2, 3, 4)]
    even = part[:3]
    odd = [
        jnp.where(left, turned[0], turned[1]), jnp.where(left, turned[1], turned[2]), turned[2],
    ]
    for k in range(3):
        square[k, pl.ds(0, count, stride=2), :] = even[k]
        square[k, pl.ds(1, count, stride=2), :] = odd[k]


def flatten_out(square, flat):
    count = square.shape[1] // 2
    left = lax.broadcasted_iota(jnp.int32, (count, 128), 1) < 64
    even = [square[k, pl.ds(0, count, stride=2), :] for k in range(3)]
    odd = [square[k, pl.ds(1, count, stride=2), :] for k in range(3)]
    turned = [pltpu.roll(values, 64, 1) for values in odd]
    part = [
        even[0], even[1], jnp.where(left, even[2], turned[0]),
        jnp.where(left, turned[0], turned[1]), jnp.where(left, turned[1], turned[2]),
    ]
    for k in range(5):
        flat[pl.ds(k, count, stride=5), :] = part[k]


def update_kernel(
    all_clips, enc_chunks, dec_chunks, grad_p, grad_b, totals,
    par, pmom, pavg, bok, bmom, bavg,
    par_new, pmom_new, pavg_new, bok_new, bmom_new, bavg_new, loss, count,
):
    loss[0, 0] = totals[0, 0]
    count[0, 0] = totals[0, 1]
    frames = totals[0:1, 1:2]
    root = math.sqrt(131.0 * all_clips)
    where = lax.axis_index("dp") * par.shape[0] + lax.broadcasted_iota(jnp.int32, par.shape, 0)
    rate = root * jnp.where(
        where < enc_chunks, ENC_RATE,
        jnp.where(where < enc_chunks + dec_chunks, DEC_RATE, OUT_RATE),
    )

    def write(grad, rate, old, mom, avg, new_ref, mom_ref, avg_ref):
        grad = grad[...] / frames
        mom_new = MOMENTUM * mom[...] + grad
        new = old[...] - rate * (grad + MOMENTUM * mom_new)
        new_ref[...] = new
        mom_ref[...] = mom_new
        avg_ref[...] = AVERAGE * avg[...] + (1.0 - AVERAGE) * new

    write(grad_p, rate, par, pmom, pavg, par_new, pmom_new, pavg_new)
    write(grad_b, BOOK_RATE * root * math.sqrt(CB), bok, bmom, bavg, bok_new, bmom_new, bavg_new)


def fused_kernel(
    enc_rows, dec_rows,
    aud, lens, codes, disc, score, spec, spec_t, par, bok, grad_p, grad_b, totals,
    pad, ipad, crow, mask, sig, disc_t, score_col, feat_real, mag_real,
    books_t, quant, hidden, slope, dec_t, out, out_t, d_out, loss,
    weights, land, flat, square, acc_p, stage_p, got_p, acc_b,
    one_b, two_b, three_b, one_d, two_d, three_d, one_e, two_e, three_e,
    last, stat, zstat, waves, send, recv, wave_sem,
):
    clip_count = aud.shape[0]
    width, samples = disc_t.shape[0], sig.shape[0]
    half = width // 2
    pairs = clip_count * LANES // WIDE
    thirds = [(pairs * k // 3, pairs * (k + 1) // 3) for k in range(3)]
    spot = lax.axis_index("dp")
    side = lax.axis_index("grp")
    other = 1 - side
    p_rows = par.shape[0] * 128 // width
    b_rows = bok.shape[0] * 128 // half
    out_rows = weights.shape[0] - enc_rows - dec_rows

    z, y, x = spot // 4, spot // 2 % 2, spot % 2
    mine_first = y + side * (x - y)
    mine_second = x + side * (y - x)

    def unit(level, first, second):
        return 4 * level + (2 - side) * first + (1 + side) * second

    def around(step):
        return (z + step) % 4

    first_dev = (unit(z, 1 - mine_first, mine_second), side)
    second_dev = (unit(z, mine_first, 1 - mine_second), side)
    pair_dev = (spot, other)

    def level_dev(level):
        return (unit(level, mine_first, mine_second), side)

    barrier = pltpu.get_barrier_semaphore()
    near = [first_dev, second_dev, pair_dev] + [level_dev(around(k)) for k in (1, 2, 3)]
    for device in near:
        pl.semaphore_signal(barrier, inc=1, device_id=device, device_id_type=MESH)

    def wave_copy(clip, slot):
        return pltpu.make_async_copy(aud.at[clip], waves.at[slot], wave_sem.at[slot])

    for slot in range(WAVES):
        wave_copy(slot, slot).start()
    taken = [0]

    def take(count):
        taken[0] += count
        return taken[0] - count

    def copy_to(device, src, dst, send_at, recv_at):
        return pltpu.make_async_remote_copy(
            src_ref=src, dst_ref=dst, send_sem=send.at[send_at], recv_sem=recv.at[recv_at],
            device_id=device, device_id_type=MESH,
        )

    def block(ref, rows, which):
        return ref.at[pl.ds(pl.multiple_of(which * rows, 16), rows), :]

    def p_view(which):
        rows = pl.ds(pl.multiple_of(which * p_rows, 16), p_rows)
        return weights.at[rows, lanes(side, half)]

    def b_view(which):
        return land.at[side, pl.ds(pl.multiple_of(which * b_rows, 16), b_rows), :]

    class Gather:
        def __init__(self, view):
            base = take(15)

            def make(slot, which, device):
                return copy_to(device, view(which), view(which), base + slot, base + slot)

            own = unit(z, mine_first, mine_second)
            self.levels = [make(k - 1, own, level_dev(around(k))) for k in (1, 2, 3)]
            self.firsts, self.seconds = [], []
            for k in range(4):
                here = unit(around(4 - k), mine_first, mine_second)
                there = unit(around(4 - k), 1 - mine_first, mine_second)
                self.firsts.append(make(3 + k, here, first_dev))
                self.seconds.append(make(7 + 2 * k, here, second_dev))
                self.seconds.append(make(8 + 2 * k, there, second_dev))

        def start(self):
            for copy in self.levels + [self.firsts[0], self.seconds[0]]:
                copy.start()

        def step(self, k):
            if k:
                self.levels[k - 1].wait_recv()
                self.firsts[k].start()
                self.seconds[2 * k].start()

        def step_back(self, k):
            self.firsts[k].wait_recv()
            self.seconds[2 * k + 1].start()

        def finish(self):
            for copy in self.seconds:
                copy.wait_recv()

        def drain(self):
            for copy in self.levels + self.firsts + self.seconds:
                copy.wait_send()

    class Scatter:
        def __init__(self, levels, rows, acc, stage, got, one, two, three):
            self.levels, self.rows, self.acc, self.stage, self.got = levels, rows, acc, stage, got
            self.landed = (one, two, three)
            low, count = levels[0] * 4 * rows, len(levels) * 4 * rows
            at = take(1)
            span = pl.ds(low, count)
            self.pair = copy_to(pair_dev, stage.at[span, :], got.at[span, :], at, at)
            base = take(2 * len(levels))
            self.sent_one, self.kept_one = [], []
            for i, level in enumerate(levels):
                for first in range(2):
                    slot = 2 * i + first
                    which = unit(level, first, 1 - mine_second)
                    self.sent_one.append((which, copy_to(
                        second_dev, block(stage, rows, which), one.at[slot],
                        base + slot, base + slot,
                    )))
                    self.kept_one.append(unit(level, first, mine_second))
            base = take(len(levels))
            self.sent_two, self.kept_two = [], []
            for i, level in enumerate(levels):
                which = unit(level, 1 - mine_first, mine_second)
                self.sent_two.append((which, copy_to(
                    first_dev, block(stage, rows, which), two.at[i], base + i, base + i,
                )))
                self.kept_two.append(unit(level, mine_first, mine_second))
            self.base = take(3)

        def read(self, ref, which):
            return ref[pl.ds(pl.multiple_of(which * self.rows, 16), self.rows), :]

        def put(self, ref, which, values):
            ref[pl.ds(pl.multiple_of(which * self.rows, 16), self.rows), :] = values

        def round_one(self):
            self.pair.wait()
            for which, copy in self.sent_one:
                total = self.read(self.acc, which) + self.read(self.got, which).astype(F32)
                self.put(self.stage, which, total.astype(BF))
                copy.start()
            for which in self.kept_one:
                total = self.read(self.acc, which) + self.read(self.got, which).astype(F32)
                self.put(self.acc, which, total)

        def fold(self, kept, sent, landed):
            for slot, which in enumerate(kept):
                sent[slot][1].wait()
                self.put(
                    self.acc, which, self.read(self.acc, which) + landed[slot].astype(F32)
                )

        def round_two(self):
            self.fold(self.kept_one, self.sent_one, self.landed[0])
            for which, copy in self.sent_two:
                self.put(self.stage, which, self.read(self.acc, which).astype(BF))
                copy.start()

        def level_copy(self, level, send_slot, slot):
            which = unit(level, mine_first, mine_second)
            return which, copy_to(
                level_dev(level), block(self.stage, self.rows, which), self.landed[2].at[slot],
                self.base + send_slot, self.base + slot,
            )

        def level_plan(self):
            if len(self.levels) == 4:
                return [(None, around(k), k - 1, k - 1) for k in (1, 2, 3)]
            rank = (z + 4 - self.levels[0]) % 4
            return [
                (rank != 0, self.levels[0], 0, (rank + 3) % 4),
                (rank != 1, self.levels[1], 1, (rank + 1) // 2),
            ]

        def round_three(self):
            self.fold(self.kept_two, self.sent_two, self.landed[1])
            for condition, level, send_slot, slot in self.level_plan():
                def go(level=level, send_slot=send_slot, slot=slot):
                    which, copy = self.level_copy(level, send_slot, slot)
                    self.put(self.stage, which, self.read(self.acc, which).astype(BF))
                    copy.start()

                if condition is None:
                    go()
                else:
                    pl.when(condition)(go)

        def settle(self):
            def take_in():
                total = self.read(self.acc, spot)
                for slot in range(3):
                    self.level_copy(z, slot, slot)[1].wait_recv()
                    total = total + self.landed[2][slot].astype(F32)
                self.put(self.acc, spot, total)

            for condition, level, send_slot, slot in self.level_plan():
                def gone(level=level, send_slot=send_slot, slot=slot):
                    self.level_copy(level, send_slot, slot)[1].wait_send()

                if condition is None:
                    gone()
                else:
                    pl.when(condition)(gone)
            if len(self.levels) == 4:
                take_in()
            else:
                pl.when((z + 4 - self.levels[0]) % 4 < 2)(take_in)

    for j in range(2):
        spots = pl.ds(pl.multiple_of(side * half + j * 128, 128), 128)
        weights[pl.ds(pl.multiple_of(spot * p_rows, 16), p_rows), spots] = par[
            pl.ds(2 * side + j, p_rows, stride=4), :
        ].astype(BF)
        land[side, pl.ds(pl.multiple_of(spot * b_rows, 16), b_rows), cols(j)] = bok[
            pl.ds(j, b_rows, stride=2), :
        ].astype(BF)
    loss[...] = jnp.zeros_like(loss)

    pl.semaphore_wait(barrier, len(near))
    gather_b, gather_p = Gather(b_view), Gather(p_view)
    at = take(2)
    swap_b = copy_to(pair_dev, land.at[side], land.at[side], at, at)
    span = weights.at[:, lanes(side, half)]
    swap_p = copy_to(pair_dev, span, span, at + 1, at + 1)

    gather_b.start()
    disc_t[...] = jnp.transpose(disc[...])
    score_col[...] = jnp.transpose(jnp.broadcast_to(score[...], (128, score.shape[1])))

    def fetch(clip):
        wave_copy(clip, clip % WAVES).wait()
        return waves.at[clip % WAVES]

    def free(clip):
        @pl.when(clip + WAVES < clip_count)
        def _():
            wave_copy(clip + WAVES, clip % WAVES).start()

    load_signal(clip_count, side, fetch, free, lens, codes, pad, ipad, crow, mask, sig)
    gather_b.step_back(0)
    gather_b.step(1)
    gather_p.start()
    real_args = (sig, disc_t, spec_t, feat_real, mag_real)
    real_side(thirds[0], *real_args)
    gather_b.step_back(1)
    gather_b.step(2)
    real_side(thirds[1], *real_args)
    gather_b.step_back(2)
    gather_b.step(3)
    real_side(thirds[2], *real_args)
    gather_b.step_back(3)
    gather_p.step_back(0)
    gather_b.finish()
    swap_b.start()
    gather_p.step(1)
    books_t[side] = jnp.transpose(land[side])
    gather_p.step_back(1)
    swap_b.wait()
    books_t[other] = jnp.transpose(land[other])
    gather_b.drain()
    pick(thirds[0], crow, mask, books_t, quant, hidden)
    gather_p.step(2)
    gather_p.step_back(2)
    pick(thirds[1], crow, mask, books_t, quant, hidden)
    gather_p.step(3)
    gather_p.step_back(3)
    pick(thirds[2], crow, mask, books_t, quant, hidden)
    gather_p.finish()
    swap_p.start()
    swap_p.wait()
    gather_p.drain()

    enc = weights.at[0:enc_rows, :]
    dec = weights.at[enc_rows : enc_rows + dec_rows, :]
    enc_t = dec_t.at[:, 0:enc_rows]
    enc_t[...] = jnp.transpose(enc[...])
    encode((0, pairs), enc_t, sig, quant, hidden, mask, slope, loss)

    d_dec = feat_real
    stage_b, got_b = land.at[0], land.at[1]
    scatter_b = Scatter((0, 1, 2, 3), b_rows, acc_b, stage_b, got_b, one_b, two_b, three_b)

    def far_books(level, carry):
        rows = pl.ds(pl.multiple_of(other * half, half), half)
        values = book_grad(clip_count, crow, slope, 2 * other + level, rows)
        stage_b[lanes(level, CB), :] = values.astype(BF)
        return carry

    def near_books(level, carry):
        rows = pl.ds(pl.multiple_of(side * half, half), half)
        acc_b[lanes(level, CB), :] = book_grad(clip_count, crow, slope, 2 * side + level, rows)
        return carry

    lax.fori_loop(0, 2, far_books, 0)
    scatter_b.pair.start()
    lax.fori_loop(0, 2, near_books, 0)
    scatter_b.round_one()

    dec_t[...] = jnp.transpose(dec[...])
    for j in range(4):
        flat[pl.ds(j, out_rows, stride=4), :] = weights[
            enc_rows + dec_rows :, cols(j)
        ].astype(F32)
    unflatten_out(flat, square)
    edges = [(k, k * 128, min(k * 128 + 128, samples)) for k in range(3)]
    for k, start, stop in edges:
        out[:, start:stop] = square[k, :, 0 : stop - start].astype(BF)
    out_t[...] = jnp.transpose(out[...])
    decode_refs = (
        quant, dec_t, out, out_t, mask, sig, spec, spec_t, disc, disc_t, score_col,
        feat_real, mag_real, hidden, d_out, d_dec,
    )
    decode(thirds[0], decode_refs, loss)
    scatter_b.round_two()
    decode(thirds[1], decode_refs, loss)
    scatter_b.round_three()
    decode(thirds[2], decode_refs, loss)

    grad_out = dot_nt(hidden[...], d_out[...])
    for k, start, stop in edges:
        square[k, :, 0 : stop - start] = grad_out[:, start:stop]
    flatten_out(square, flat)
    low = enc_rows + dec_rows
    for j in range(2):
        near_part = flat[pl.ds(2 * side + j, out_rows, stride=4), :]
        far_part = flat[pl.ds(2 * other + j, out_rows, stride=4), :]
        acc_p[low : low + out_rows, cols(j)] = near_part
        stage_p[low : low + out_rows, cols(j)] = far_part.astype(BF)

    scatter_d = Scatter((2, 3), p_rows, acc_p, stage_p, got_p, one_d, two_d, three_d)
    scatter_e = Scatter((0, 1), p_rows, acc_p, stage_p, got_p, one_e, two_e, three_e)
    near_rows = pl.ds(pl.multiple_of(side * half, half), half)
    far_rows = pl.ds(pl.multiple_of(other * half, half), half)
    for k, shift in ((1, None), (0, before), (2, after)):
        values = quant
        if shift is not None:
            values = hidden
            hidden[...] = shift(quant[...])
        rows = slice(enc_rows + k * width, enc_rows + (k + 1) * width)
        stage_p[rows, :] = dot_nt(values[...], d_dec[far_rows, :]).astype(BF)
        if k == 2:
            scatter_d.pair.start()
            scatter_b.settle()
        acc_p[rows, :] = dot_nt(values[...], d_dec[near_rows, :])
    d_out[...] = before(sig[...])
    hidden[0:samples, :] = after(sig[...])
    shifted = (d_out, sig, hidden.at[0:samples, :])
    scatter_d.round_one()

    valid = jnp.sum(mask[...])
    lost = jnp.sum(loss[...])
    first_lane = lax.broadcasted_iota(jnp.int32, (8, 128), 1) == 0
    stat[0] = jnp.where(first_lane, lost, valid)
    at = take(6)
    swaps = [
        copy_to(device, stat.at[2 * k], stat.at[2 * k + 1], at + k, at + k)
        for k, device in enumerate((pair_dev, first_dev, second_dev))
    ]
    level_swaps = [
        copy_to(level_dev(around(k)), zstat.at[z], zstat.at[z], at + 2 + k, at + 2 + k)
        for k in (1, 2, 3)
    ]
    swaps[0].start()
    latent_args = (dec, d_dec, mask, slope, slope)
    latent_back(thirds[0], *latent_args)
    scatter_d.round_two()
    swaps[0].wait()
    stat[2] = stat[0] + stat[1]
    swaps[1].start()
    latent_back(thirds[1], *latent_args)
    swaps[1].wait()
    stat[4] = stat[2] + stat[3]
    swaps[2].start()
    scatter_d.round_three()
    latent_back(thirds[2], *latent_args)
    swaps[2].wait()
    zstat[z] = stat[4] + stat[5]
    for copy in level_swaps:
        copy.start()
    for k, values in enumerate(shifted):
        rows = slice(k * samples, (k + 1) * samples)
        stage_p[rows, :] = dot_nt(values[...], slope[far_rows, :]).astype(BF)
    scatter_e.pair.start()
    for k, values in enumerate(shifted):
        rows = slice(k * samples, (k + 1) * samples)
        acc_p[rows, :] = dot_nt(values[...], slope[near_rows, :])
    scatter_d.settle()
    scatter_e.round_one()

    for copy in level_swaps:
        copy.wait()
    totals[...] = (zstat[0] + zstat[1]) + (zstat[2] + zstat[3])
    own_b = pl.ds(pl.multiple_of(spot * b_rows, 16), b_rows)
    for j in range(2):
        grad_b[pl.ds(j, b_rows, stride=2), :] = acc_b[own_b, cols(j)]
    scatter_e.round_two()
    scatter_e.round_three()
    scatter_e.settle()

    own_p = pl.ds(pl.multiple_of(spot * p_rows, 16), p_rows)
    at = take(1)
    swap = copy_to(pair_dev, acc_p.at[own_p, :], last, at, at)
    swap.start()
    for j in range(2):
        grad_p[pl.ds(2 * side + j, p_rows, stride=4), :] = acc_p[own_p, cols(j)]
    swap.wait()
    for j in range(2):
        grad_p[pl.ds(2 * other + j, p_rows, stride=4), :] = last[:, cols(j)]
    assert taken[0] <= COPIES


def fused(
    audio, lengths, codes, disc_weight, disc_score, params, params_mom, params_avg, books,
    books_mom, books_avg,
):
    clip_count, _, samples = audio.shape
    width = disc_weight.shape[1]
    half = width // 2
    chips = lax.axis_size("dp")
    total = clip_count * LANES
    table = spectral_table(samples)
    p_rows, b_rows = params.shape[0] // width, books.shape[1] // half
    all_rows, book_rows = p_rows * chips, b_rows * chips
    vmem = pl.BlockSpec(memory_space=pltpu.VMEM)
    smem = pl.BlockSpec(memory_space=pltpu.SMEM)
    p_shape = (params.shape[0] // 128, 128)
    b_shape = (books.shape[1] // 128, 128)
    all_clips = clip_count * chips * lax.axis_size("grp")
    weights = [value.reshape(p_shape) for value in (params, params_mom, params_avg)]
    tables = [value.reshape(b_shape) for value in (books, books_mom, books_avg)]
    grad_shapes = [jax.ShapeDtypeStruct(p_shape, F32), jax.ShapeDtypeStruct(b_shape, F32)]
    grads = pl.pallas_call(
        functools.partial(fused_kernel, 3 * samples, 3 * width),
        out_shape=grad_shapes + [jax.ShapeDtypeStruct((8, 128), F32)],
        in_specs=[pl.BlockSpec(memory_space=pl.ANY), smem] + [vmem] * 7,
        out_specs=[vmem] * 3,
        scratch_shapes=[
            pltpu.VMEM((samples, LANES), BF),
            pltpu.VMEM((8, LANES), jnp.int32),
            pltpu.VMEM((8, total), jnp.int32),
            pltpu.VMEM((1, total), F32),
            pltpu.VMEM((samples, total), BF),
            pltpu.VMEM((width, 3 * samples), BF),
            pltpu.VMEM((width, 128), F32),
            pltpu.VMEM((width, total), BF),
            pltpu.VMEM((samples // 2, total), F32),
            pltpu.VMEM((2, half, 2 * CB), BF),
            pltpu.VMEM((width, total), BF),
            pltpu.VMEM((width, total), BF),
            pltpu.VMEM((width, total), BF),
            pltpu.VMEM((width, 3 * width), BF),
            pltpu.VMEM((width, samples), BF),
            pltpu.VMEM((samples, width), BF),
            pltpu.VMEM((samples, total), BF),
            pltpu.VMEM((1, WIDE), F32),
            pltpu.VMEM((all_rows, width), BF),
            pltpu.VMEM((2, book_rows, half), BF),
            pltpu.VMEM((width * samples // 128, 128), F32),
            pltpu.VMEM((3, width, 128), F32),
            pltpu.VMEM((all_rows, half), F32),
            pltpu.VMEM((all_rows, half), BF),
            pltpu.VMEM((all_rows, half), BF),
            pltpu.VMEM((book_rows, half), F32),
            pltpu.VMEM((8, b_rows, half), BF),
            pltpu.VMEM((4, b_rows, half), BF),
            pltpu.VMEM((3, b_rows, half), BF),
            pltpu.VMEM((4, p_rows, half), BF),
            pltpu.VMEM((2, p_rows, half), BF),
            pltpu.VMEM((3, p_rows, half), BF),
            pltpu.VMEM((4, p_rows, half), BF),
            pltpu.VMEM((2, p_rows, half), BF),
            pltpu.VMEM((3, p_rows, half), BF),
            pltpu.VMEM((p_rows, half), F32),
            pltpu.VMEM((6, 8, 128), F32),
            pltpu.VMEM((4, 8, 128), F32),
            pltpu.VMEM((WAVES, samples, audio.shape[1]), BF),
            pltpu.SemaphoreType.DMA((COPIES,)),
            pltpu.SemaphoreType.DMA((COPIES,)),
            pltpu.SemaphoreType.DMA((WAVES,)),
        ],
        compiler_params=pltpu.CompilerParams(
            vmem_limit_bytes=VMEM_LIMIT, collective_id=0, has_side_effects=True
        ),
        name="train_step",
    )(
        jnp.swapaxes(audio, 1, 2), lengths, codes, disc_weight, disc_score.reshape(1, width),
        jnp.asarray(table, BF), jnp.asarray(table.T, BF), weights[0], tables[0],
    )
    outs = pl.pallas_call(
        functools.partial(
            update_kernel, all_clips, 3 * samples * width // 128, 3 * width * width // 128
        ),
        out_shape=[grad_shapes[0]] * 3 + [grad_shapes[1]] * 3
        + [jax.ShapeDtypeStruct((1, 1), F32)] * 2,
        in_specs=[vmem] * 9,
        out_specs=[vmem] * 6 + [smem] * 2,
        name="train_update",
    )(*grads, *weights, *tables)
    return (
        *(value.reshape(params.shape) for value in outs[:3]),
        *(value.reshape(books.shape) for value in outs[3:6]),
        outs[6].reshape(()),
        outs[7].reshape(()),
    )


def solution(mesh):
    in_specs = (
        P(("dp", "grp"), None, None), P("dp"), P(None, None, "dp", None), P(), P(), P("dp"),
        P("dp"), P("dp"), P("grp", "dp"), P("grp", "dp"), P("grp", "dp"),
    )
    out_specs = (
        P("dp"), P("dp"), P("dp"), P("grp", "dp"), P("grp", "dp"), P("grp", "dp"), P(), P(),
    )
    body = fused if mesh.shape["dp"] == math.prod(CHIPS) else shards
    return jax.shard_map(body, mesh=mesh, in_specs=in_specs, out_specs=out_specs, check_vma=False)
```

```python
import functools
import math

import jax
import jax.numpy as jnp
import numpy as np
from jax import lax
from jax.experimental import pallas as pl
from jax.experimental.pallas import tpu as pltpu
from jax.sharding import PartitionSpec as P

BF = jnp.bfloat16
F32 = jnp.float32
MOMENTUM = 0.9
AVERAGE = 0.99
LANES = 256
CB = 1024
WIDE = 512
VMEM_LIMIT = 56 << 20


def spectral_table(samples):
    spots = np.arange(samples)[:, None]
    bins = np.arange(samples // 2)[None, :]
    turns = (spots * bins % samples) * (2.0 * math.pi / samples)
    window = 0.5 - 0.5 * np.cos((spots + 0.5) * (2.0 * math.pi / samples))
    table = np.concatenate([window * np.cos(turns), window * np.sin(turns)], axis=1)
    return (table * math.sqrt(2.0 / samples)).astype(np.float32)


def dot(left, right):
    return jnp.dot(left, right, preferred_element_type=F32)


def dot_nt(left, right):
    return lax.dot_general(left, right, (((1,), (1,)), ((), ())), preferred_element_type=F32)


def lanes(index, width):
    return pl.ds(pl.multiple_of(index * width, width), width)


def loop(bounds, step, hooks):
    hooks = dict(hooks)

    def body(index, carry):
        step(index)
        for after_index, hook in hooks.items():
            pl.when(index == after_index)(hook)
        return carry

    lax.fori_loop(*bounds, body, 0)


def col_sum(values):
    return jnp.sum(values, axis=0, keepdims=True)


def before(values):
    return pltpu.roll(values, 1, 1)


def after(values):
    return pltpu.roll(values, values.shape[1] - 1, 1)


def stack_three(values):
    return jnp.concatenate([before(values), values, after(values)], axis=0)


def silu_parts(values):
    sigmoid = 0.5 * jnp.tanh(0.5 * values) + 0.5
    return values * sigmoid, sigmoid * (1.0 + values * (1.0 - sigmoid))


def silu(values):
    return values * (0.5 * jnp.tanh(0.5 * values) + 0.5)


def load_signal(
    clip_count, side, fetch, free, lens, codes, pad, ipad, crow, mask, sig, hooks=()
):
    slots = codes.shape[3]
    pad[...] = jnp.zeros_like(pad)
    ipad[...] = jnp.full(ipad.shape, -1, jnp.int32)
    spots = lax.broadcasted_iota(jnp.int32, (1, LANES), 1)

    def step(clip):
        here = lanes(clip, LANES)
        row = side * clip_count + clip
        own = (spots < lens[row]).astype(F32)
        mask[:, here] = own
        for which in range(4):
            ipad[which : which + 1, 0:slots] = codes[which // 2, which % 2, pl.ds(row, 1), :]
        crow[:, here] = ipad[...]
        pad[:, 0:slots] = fetch(clip)[...]
        free(clip)
        wave = pad[...].astype(F32) * own
        sig[:, here] = wave.astype(BF)

    loop((0, clip_count), step, hooks)


def real_side(pairs, sig, disc_t, spec_t, feat_real, mag_real, hooks=()):
    samples = spec_t.shape[0]
    half = samples // 2

    def step(pair):
        here = lanes(pair, WIDE)
        wave = sig[:, here]
        feat_real[:, here] = silu(dot(disc_t[...], stack_three(wave))).astype(BF)
        spec = dot(spec_t[...], wave)
        norm = spec[:half] * spec[:half] + spec[half:] * spec[half:] + 1.0
        mag_real[:, here] = jnp.sqrt(norm)

    loop(pairs, step, hooks)


def onehot(crow, which, here, count):
    entries = lax.broadcasted_iota(jnp.int32, (CB, count), 0)
    return (entries == crow[pl.ds(which, 1), here]).astype(F32).astype(BF)


def encode(pairs, enc_t, sig, latent, hooks=()):
    def step(pair):
        here = lanes(pair, WIDE)
        latent[:, here] = dot(enc_t[...], stack_three(sig[:, here])).astype(BF)

    loop(pairs, step, hooks)


def pick(pairs, crow, mask, books_t, quant, slope, loss, hooks=()):
    half = books_t.shape[1]
    width = 2 * half

    def step(pair):
        here = lanes(pair, WIDE)
        own = mask[:, here]
        lost = jnp.zeros_like(own)
        for group in range(2):
            rows = slice(group * half, (group + 1) * half)
            hot = jnp.concatenate(
                [onehot(crow, 2 * group, here, WIDE), onehot(crow, 2 * group + 1, here, WIDE)], 0
            )
            value = dot(books_t[group], hot)
            quant[rows, here] = (value * own).astype(BF)
            gap = (slope[rows, here].astype(F32) - value) * own
            lost += col_sum(gap * gap)
            slope[rows, here] = (gap * (-2.0 / width)).astype(BF)
        loss[...] += lost * (1.0 / width)

    loop(pairs, step, hooks)


def book_grad(clip_count, crow, slope, which, rows):
    total = None
    chunk = 4 * LANES
    for part in range(clip_count * LANES // chunk):
        here = pl.ds(part * chunk, chunk)
        term = dot_nt(onehot(crow, which, here, chunk), slope[rows, here])
        total = term if total is None else total + term
    return total


def decode(pairs, refs, loss, hooks=()):
    (quant, dec_t, out, out_t, mask, sig, spec, spec_t, disc, disc_t, score_col) = refs[:11]
    (feat_real, mag_real, hidden, d_out, d_dec) = refs[11:]
    samples = spec.shape[0]
    width = hidden.shape[0]
    half = samples // 2

    def step(pair):
        here = lanes(pair, WIDE)
        own = mask[:, here]
        pre_dec = dot(dec_t[...], stack_three(quant[:, here]))
        act, act_slope = silu_parts(pre_dec)
        act = act.astype(BF)
        hidden[:, here] = act
        tanh_out = jnp.tanh(dot(out_t[...], act))
        made = tanh_out * own
        wave_gap = made - sig[:, here].astype(F32)
        norm = wave_gap * wave_gap + 1.0
        root = lax.rsqrt(norm)
        lost = col_sum(norm * root - 1.0) * (1.0 / samples)
        d_made = wave_gap * root * (1.0 / samples)
        made_low = made.astype(BF)

        spec_fake = dot(spec_t[...], made_low)
        real_part, imag_part = spec_fake[:half], spec_fake[half:]
        norm = real_part * real_part + imag_part * imag_part + 1.0
        root = lax.rsqrt(norm)
        spec_gap = norm * root - mag_real[:, here]
        norm = spec_gap * spec_gap + 1.0
        gap_root = lax.rsqrt(norm)
        lost += col_sum(norm * gap_root - 1.0) * (1.0 / samples)
        d_mag = spec_gap * gap_root * root * (1.0 / samples)
        d_spec = jnp.concatenate([d_mag * real_part, d_mag * imag_part], axis=0).astype(BF)
        d_made += dot(spec[...], d_spec)

        pre_fake = dot(disc_t[...], stack_three(made_low))
        feat_fake, feat_slope = silu_parts(pre_fake)
        weight = jnp.concatenate([score_col[...]] * (WIDE // 128), axis=1)
        miss = 1.0 - col_sum(feat_fake * weight)
        feat_gap = feat_fake - feat_real[:, here].astype(F32)
        norm = feat_gap * feat_gap + 1.0
        root = lax.rsqrt(norm)
        lost += own * (miss * miss + col_sum(norm * root - 1.0) * (1.0 / width))
        d_feat = (-2.0 * own * miss) * weight + (own * (1.0 / width)) * (feat_gap * root)
        d_fake = (d_feat * feat_slope).astype(BF)
        back = dot(disc[...], d_fake)
        d_made += after(back[:samples]) + back[samples : 2 * samples] + before(back[2 * samples :])

        d_pre_out = (d_made * own * (1.0 - tanh_out * tanh_out)).astype(BF)
        d_out[:, here] = d_pre_out
        d_dec[:, here] = (dot(out[...], d_pre_out) * act_slope).astype(BF)
        loss[...] += lost

    loop(pairs, step, hooks)


def latent_back(pairs, dec, d_dec, mask, slope, d_latent, hooks=()):
    width = d_dec.shape[0]

    def step(pair):
        here = lanes(pair, WIDE)
        back = dot(dec[...], d_dec[:, here])
        joined = after(back[:width]) + back[width : 2 * width] + before(back[2 * width :])
        joined = joined.astype(BF).astype(F32) * mask[:, here]
        d_latent[:, here] = (joined - slope[:, here].astype(F32)).astype(BF)

    loop(pairs, step, hooks)


def local_kernel(
    aud, lens, codes, disc, score, spec, spec_t, enc, dec, out, books,
    g_enc, g_dec, g_out, g_books, loss_out,
    pad, ipad, crow, mask, sig, disc_t, score_col, feat_real, mag_real,
    books_t, quant, hidden, enc_t, slope, dec_t, out_t, d_out, d_dec, loss,
):
    clip_count = aud.shape[0]
    pairs = (0, clip_count * LANES // WIDE)
    side = lax.axis_index("grp")
    loss[...] = jnp.zeros_like(loss)
    disc_t[...] = jnp.transpose(disc[...])
    score_col[...] = jnp.transpose(jnp.broadcast_to(score[...], (128, score.shape[1])))
    load_signal(
        clip_count, side, lambda clip: aud.at[clip], lambda clip: None, lens, codes, pad, ipad,
        crow, mask, sig,
    )
    real_side(pairs, sig, disc_t, spec_t, feat_real, mag_real)
    for group in range(2):
        books_t[group] = jnp.transpose(books[group])
    enc_t[...] = jnp.transpose(enc[...])
    dec_t[...] = jnp.transpose(dec[...])
    out_t[...] = jnp.transpose(out[...])
    encode(pairs, enc_t, sig, slope)
    pick(pairs, crow, mask, books_t, quant, slope, loss)

    def book_step(which, carry):
        rows = pl.ds(pl.multiple_of(which // 2 * 256, 256), 256)
        g_books[which] = book_grad(clip_count, crow, slope, which, rows)
        return carry

    lax.fori_loop(0, 4, book_step, 0)
    decode(
        pairs,
        (quant, dec_t, out, out_t, mask, sig, spec, spec_t, disc, disc_t, score_col,
         feat_real, mag_real, hidden, d_out, d_dec),
        loss,
    )
    g_out[...] = dot_nt(hidden[...], d_out[...])

    width = quant.shape[0]
    for part, shift in enumerate((before, lambda values: values, after)):
        g_dec[part * width : (part + 1) * width, :] = dot_nt(shift(quant[...]), d_dec[...])
    latent_back(pairs, dec, d_dec, mask, slope, hidden)

    samples = sig.shape[0]
    for part, shift in enumerate((before, lambda values: values, after)):
        g_enc[part * samples : (part + 1) * samples, :] = dot_nt(shift(sig[...]), hidden[...])
    loss_out[...] = loss[...]


def local_call(audio_t, lengths, codes, disc, score, enc, dec, out, books):
    clip_count, samples, _ = audio_t.shape
    width = disc.shape[1]
    total = clip_count * LANES
    table = spectral_table(samples)
    vmem = pl.BlockSpec(memory_space=pltpu.VMEM)
    smem = pl.BlockSpec(memory_space=pltpu.SMEM)
    return pl.pallas_call(
        local_kernel,
        out_shape=(
            jax.ShapeDtypeStruct((3 * samples, width), F32),
            jax.ShapeDtypeStruct((3 * width, width), F32),
            jax.ShapeDtypeStruct((width, samples), F32),
            jax.ShapeDtypeStruct((4, CB, width // 2), F32),
            jax.ShapeDtypeStruct((1, WIDE), F32),
        ),
        in_specs=[vmem, smem] + [vmem] * 9,
        out_specs=[vmem] * 5,
        scratch_shapes=[
            pltpu.VMEM((samples, LANES), BF),
            pltpu.VMEM((8, LANES), jnp.int32),
            pltpu.VMEM((8, total), jnp.int32),
            pltpu.VMEM((1, total), F32),
            pltpu.VMEM((samples, total), BF),
            pltpu.VMEM((width, 3 * samples), BF),
            pltpu.VMEM((width, 128), F32),
            pltpu.VMEM((width, total), BF),
            pltpu.VMEM((samples // 2, total), F32),
            pltpu.VMEM((2, width // 2, 2 * CB), BF),
            pltpu.VMEM((width, total), BF),
            pltpu.VMEM((width, total), BF),
            pltpu.VMEM((width, 3 * samples), BF),
            pltpu.VMEM((width, total), BF),
            pltpu.VMEM((width, 3 * width), BF),
            pltpu.VMEM((samples, width), BF),
            pltpu.VMEM((samples, total), BF),
            pltpu.VMEM((width, total), BF),
            pltpu.VMEM((1, WIDE), F32),
        ],
        compiler_params=pltpu.CompilerParams(vmem_limit_bytes=56 << 20),
        name="train_local",
    )(
        audio_t, lengths, codes, disc, score.reshape(1, width),
        jnp.asarray(table, BF), jnp.asarray(table.T, BF), enc, dec, out, books,
    )


def shards(
    audio, lengths, codes, disc_weight, disc_score, params, params_mom, params_avg, books,
    books_mom, books_avg,
):
    clip_count, slot_count, samples = audio.shape
    width = disc_weight.shape[1]
    half_width = width // 2
    side = lax.axis_index("grp")
    shared = lax.all_gather(params.astype(BF), "dp", axis=0, tiled=True)
    table = lax.all_gather(books.astype(BF), ("grp", "dp"), axis=1, tiled=True)
    enc_size = 3 * samples * width
    dec_size = 3 * width * width
    enc_weight = shared[:enc_size].reshape(3 * samples, width)
    dec_weight = shared[enc_size : enc_size + dec_size].reshape(3 * width, width)
    out_weight = shared[enc_size + dec_size :].reshape(width, samples)
    codebook = table.reshape(2, 2 * CB, half_width)
    local_count = jnp.sum(
        lax.dynamic_slice_in_dim(lengths, side * clip_count, clip_count, 0)
    ).astype(F32)
    frame_count = lax.psum(local_count, ("dp", "grp"))
    grad_enc, grad_dec, grad_out, grad_book, lost = local_call(
        jnp.swapaxes(audio, 1, 2), lengths, codes, disc_weight, disc_score,
        enc_weight, dec_weight, out_weight, codebook,
    )
    grad_shared = jnp.concatenate(
        [grad_enc.reshape(-1), grad_dec.reshape(-1), grad_out.reshape(-1)]
    )
    grad_shared = lax.psum(grad_shared.astype(BF), "grp").astype(F32)
    grad_book = lax.psum_scatter(
        grad_book.reshape(2, -1), "grp", scatter_dimension=0, tiled=True
    )
    shared_part = lax.psum_scatter(grad_shared, "dp", scatter_dimension=0, tiled=True)
    book_part = lax.psum_scatter(grad_book, "dp", scatter_dimension=1, tiled=True)
    loss_sum = lax.psum(jnp.sum(lost), ("dp", "grp"))
    all_clips = clip_count * lax.axis_size("dp") * lax.axis_size("grp")
    root = math.sqrt(131.0 * all_clips)
    shard_length = params.shape[0]
    spots = lax.axis_index("dp") * shard_length + jnp.arange(shard_length)
    rate = (
        jnp.where(spots < enc_size, 0.65, jnp.where(spots < enc_size + dec_size, 0.14, 0.2)) * root
    )
    shared_grad = shared_part / frame_count
    mom_new = MOMENTUM * params_mom + shared_grad
    param_new = params - rate * (shared_grad + MOMENTUM * mom_new)
    avg_new = AVERAGE * params_avg + (1.0 - AVERAGE) * param_new
    book_rate = 3.9 * math.sqrt(131.0 * all_clips * CB)
    book_grad_mean = book_part / frame_count
    book_mom_new = MOMENTUM * books_mom + book_grad_mean
    book_new = books - book_rate * (book_grad_mean + MOMENTUM * book_mom_new)
    book_avg_new = AVERAGE * books_avg + (1.0 - AVERAGE) * book_new
    return (
        param_new, mom_new, avg_new, book_new, book_mom_new, book_avg_new, loss_sum, frame_count,
    )


MESH = pl.DeviceIdType.MESH
ENC_RATE, DEC_RATE, OUT_RATE, BOOK_RATE = 0.65, 0.14, 0.2, 3.9
CHIPS = (4, 2, 2)
SENDS, ARRIVALS = 15, 71
WAVES = 4


def cols(index, width=128):
    return slice(index * width, (index + 1) * width)


def unflatten_out(flat, square):
    count = square.shape[1] // 2
    left = lax.broadcasted_iota(jnp.int32, (count, 128), 1) < 64
    part = [flat[pl.ds(k, count, stride=5), :] for k in range(5)]
    turned = [pltpu.roll(part[k], 64, 1) for k in (2, 3, 4)]
    even = part[:3]
    odd = [
        jnp.where(left, turned[0], turned[1]), jnp.where(left, turned[1], turned[2]), turned[2],
    ]
    for k in range(3):
        square[k, pl.ds(0, count, stride=2), :] = even[k]
        square[k, pl.ds(1, count, stride=2), :] = odd[k]


def flatten_out(square, flat):
    count = square.shape[1] // 2
    left = lax.broadcasted_iota(jnp.int32, (count, 128), 1) < 64
    even = [square[k, pl.ds(0, count, stride=2), :] for k in range(3)]
    odd = [square[k, pl.ds(1, count, stride=2), :] for k in range(3)]
    turned = [pltpu.roll(values, 64, 1) for values in odd]
    part = [
        even[0], even[1], jnp.where(left, even[2], turned[0]),
        jnp.where(left, turned[0], turned[1]), jnp.where(left, turned[1], turned[2]),
    ]
    for k in range(5):
        flat[pl.ds(k, count, stride=5), :] = part[k]


def update_kernel(
    all_clips, enc_chunks, dec_chunks, grad_p, grad_b, totals,
    par, pmom, pavg, bok, bmom, bavg,
    par_new, pmom_new, pavg_new, bok_new, bmom_new, bavg_new, loss, count,
):
    loss[0, 0] = totals[0, 0]
    count[0, 0] = totals[0, 1]
    frames = totals[0:1, 1:2]
    root = math.sqrt(131.0 * all_clips)
    where = lax.axis_index("dp") * par.shape[0] + lax.broadcasted_iota(jnp.int32, par.shape, 0)
    rate = root * jnp.where(
        where < enc_chunks, ENC_RATE,
        jnp.where(where < enc_chunks + dec_chunks, DEC_RATE, OUT_RATE),
    )

    def write(grad, rate, old, mom, avg, new_ref, mom_ref, avg_ref):
        grad = grad[...] / frames
        mom_new = MOMENTUM * mom[...] + grad
        new = old[...] - rate * (grad + MOMENTUM * mom_new)
        new_ref[...] = new
        mom_ref[...] = mom_new
        avg_ref[...] = AVERAGE * avg[...] + (1.0 - AVERAGE) * new

    write(grad_p, rate, par, pmom, pavg, par_new, pmom_new, pavg_new)
    write(grad_b, BOOK_RATE * root * math.sqrt(CB), bok, bmom, bavg, bok_new, bmom_new, bavg_new)


def fused_kernel(
    enc_rows, dec_rows,
    aud, lens, codes, disc, score, spec, spec_t, par, bok, grad_p, grad_b, totals,
    pad, ipad, crow, mask, sig, disc_t, score_col, feat_real, mag_real,
    books_t, quant, hidden, slope, dec_t, out, out_t, d_out, loss,
    weights, land, flat, square, acc_p, stage_p, got_p, acc_b,
    one_b, two_b, three_b, one_p, two_p, three_p,
    last, stat, zstat, waves, send, recv, wave_sem,
):
    clip_count = aud.shape[0]
    width, samples = disc_t.shape[0], sig.shape[0]
    half = width // 2
    pairs = clip_count * LANES // WIDE
    spot = lax.axis_index("dp")
    side = lax.axis_index("grp")
    other = 1 - side
    p_rows = par.shape[0] * 128 // width
    b_rows = bok.shape[0] * 128 // half
    out_rows = weights.shape[0] - enc_rows - dec_rows

    z, y, x = spot // 4, spot // 2 % 2, spot % 2
    mine_first = y + side * (x - y)
    mine_second = x + side * (y - x)

    def unit(level, first, second):
        return 4 * level + (2 - side) * first + (1 + side) * second

    def around(step):
        return (z + step) % 4

    first_dev = (unit(z, 1 - mine_first, mine_second), side)
    second_dev = (unit(z, mine_first, 1 - mine_second), side)
    pair_dev = (spot, other)

    def level_dev(level):
        return (unit(level, mine_first, mine_second), side)

    barrier = pltpu.get_barrier_semaphore()
    near = [first_dev, second_dev, pair_dev] + [level_dev(around(k)) for k in (1, 2, 3)]
    for device in near:
        pl.semaphore_signal(barrier, inc=1, device_id=device, device_id_type=MESH)

    def wave_copy(clip, slot):
        return pltpu.make_async_copy(aud.at[clip], waves.at[slot], wave_sem.at[slot])

    for slot in range(WAVES):
        wave_copy(slot, slot).start()
    taken = {"send": 0, "recv": 0}

    def take(kind, count=1):
        taken[kind] += count
        return taken[kind] - count

    def copy_to(device, src, dst, send_at, recv_at):
        return pltpu.make_async_remote_copy(
            src_ref=src, dst_ref=dst, send_sem=send.at[send_at], recv_sem=recv.at[recv_at],
            device_id=device, device_id_type=MESH,
        )

    def block(ref, rows, which):
        return ref.at[pl.ds(pl.multiple_of(which * rows, 16), rows), :]

    def p_view(which, count=1):
        rows = pl.ds(pl.multiple_of(which * p_rows, 16), count * p_rows)
        return weights.at[rows, lanes(side, half)]

    def b_view(which, count=1):
        rows = pl.ds(pl.multiple_of(which * b_rows, 16), count * b_rows)
        return land.at[side, rows, :]

    def held(span, which, run):
        if span is None:
            run()
        else:
            pl.when((which >= span[0]) & (which < span[1]))(run)

    def wait_sent(ref, at):
        copy_to(pair_dev, ref, ref, at, 0).wait_send()

    def wait_got(ref, at):
        copy_to(pair_dev, ref, ref, 0, at).wait_recv()

    class Slots:
        def __init__(self):
            self.sent = take("send")
            self.got = take("recv", 15)

    class Gather:
        def __init__(self, view, span, slots):
            self.view, self.span, self.slots = view, span, slots
            self.swap_sent, self.swap_got = take("send"), take("recv")

            def make(slot, which, device):
                return copy_to(
                    device, view(which), view(which), slots.sent, slots.got + slot
                )

            self.levels, self.firsts, self.seconds = [], [], []
            for k in range(4):
                here = unit(around(4 - k), mine_first, mine_second)
                there = unit(around(4 - k), 1 - mine_first, mine_second)
                if k:
                    self.levels.append(make(k - 1, spot, level_dev(around(k))))
                self.firsts.append(make(3 + k, here, first_dev))
                self.seconds.append(
                    [make(7 + 2 * k, here, second_dev), make(8 + 2 * k, there, second_dev)]
                )

        def swap(self, which):
            copy_to(
                pair_dev, self.view(which), self.view(which), self.swap_sent, self.swap_got
            ).start()

        def start(self):
            def run():
                for copy in self.levels + [self.firsts[0], self.seconds[0][0]]:
                    copy.start()
                self.swap(spot)

            held(self.span, spot, run)

        def step(self):
            for k in (1, 2, 3):
                which = unit(around(4 - k), mine_first, mine_second)

                def run(k=k, which=which):
                    self.levels[k - 1].wait_recv()
                    self.firsts[k].start()
                    self.seconds[k][0].start()
                    self.swap(which)

                held(self.span, which, run)

        def back(self, ks):
            for k in ks:
                which = unit(around(4 - k), 1 - mine_first, mine_second)

                def run(k=k, which=which):
                    self.firsts[k].wait_recv()
                    self.seconds[k][1].start()
                    self.swap(which)

                held(self.span, which, run)

        def finish(self, ks):
            for k in ks:
                for slot, first in enumerate((mine_first, 1 - mine_first)):
                    which = unit(around(4 - k), first, 1 - mine_second)

                    def run(k=k, slot=slot, which=which):
                        self.seconds[k][slot].wait_recv()
                        self.swap(which)

                    held(self.span, which, run)

        def settle(self):
            wait_got(self.view(*self.span_units()), self.swap_got)
            wait_sent(self.view(*self.span_units()), self.swap_sent)

        def span_units(self):
            start, stop = self.span or (0, 16)
            return start, stop - start

    class Scatter:
        def __init__(self, span, rows, acc, stage, got, landed, slots):
            self.span, self.rows, self.acc, self.stage, self.got = span, rows, acc, stage, got
            self.landed, self.slots = landed, slots
            start, stop = span or (0, 16)
            self.levels = list(range(start // 4, (stop + 3) // 4))
            both_rows = pl.ds(start * rows, (stop - start) * rows)
            self.pair = copy_to(
                pair_dev, stage.at[both_rows, :], got.at[both_rows, :], take("send"), take("recv")
            )
            one, two, three = landed
            self.sent_one, self.kept_one, self.sent_two, self.kept_two = [], [], [], []
            for level in self.levels:
                for first in range(2):
                    slot = 2 * level + first
                    which = unit(level, first, 1 - mine_second)
                    self.sent_one.append((which, copy_to(
                        second_dev, block(stage, rows, which), one.at[slot],
                        slots.sent, slots.got + slot,
                    )))
                    self.kept_one.append((unit(level, first, mine_second), one, slot))
                which = unit(level, 1 - mine_first, mine_second)
                self.sent_two.append((which, copy_to(
                    first_dev, block(stage, rows, which), two.at[level],
                    slots.sent, slots.got + 8 + level,
                )))
                self.kept_two.append((unit(level, mine_first, mine_second), two, level))

        def read(self, ref, which):
            return ref[pl.ds(pl.multiple_of(which * self.rows, 16), self.rows), :]

        def put(self, ref, which, values):
            ref[pl.ds(pl.multiple_of(which * self.rows, 16), self.rows), :] = values

        def round_one(self):
            self.pair.wait()
            for which, copy in self.sent_one:
                def run(which=which, copy=copy):
                    total = self.read(self.acc, which) + self.read(self.got, which).astype(F32)
                    self.put(self.stage, which, total.astype(BF))
                    copy.start()

                held(self.span, which, run)
            for which, _, _ in self.kept_one:
                def keep(which=which):
                    total = self.read(self.acc, which) + self.read(self.got, which).astype(F32)
                    self.put(self.acc, which, total)

                held(self.span, which, keep)

        def fold(self, kept, sent):
            for (which, landed, slot), (_, copy) in zip(kept, sent):
                def run(which=which, landed=landed, slot=slot, copy=copy):
                    copy.wait_recv()
                    self.put(
                        self.acc, which, self.read(self.acc, which) + landed[slot].astype(F32)
                    )

                held(self.span, which, run)

        def round_two(self):
            self.fold(self.kept_one, self.sent_one)
            for which, copy in self.sent_two:
                def run(which=which, copy=copy):
                    self.put(self.stage, which, self.read(self.acc, which).astype(BF))
                    copy.start()

                held(self.span, which, run)

        def round_three(self):
            self.fold(self.kept_two, self.sent_two)
            for level in self.levels:
                which = unit(level, mine_first, mine_second)
                slot = (z + 7 - level) % 4 % 3

                def run(level=level, which=which, slot=slot):
                    self.put(self.stage, which, self.read(self.acc, which).astype(BF))
                    copy_to(
                        level_dev(level), block(self.stage, self.rows, which),
                        self.landed[2].at[slot], self.slots.sent, self.slots.got + 12 + slot,
                    ).start()

                pl.when(z != level)(functools.partial(held, self.span, which, run))

        def settle(self):
            def run():
                total = self.read(self.acc, spot)
                for slot in range(3):
                    wait_got(self.landed[2].at[slot], self.slots.got + 12 + slot)
                    total = total + self.landed[2][slot].astype(F32)
                self.put(self.acc, spot, total)

            held(self.span, spot, run)

        def drain(self):
            wait_sent(self.stage.at[0 : 15 * self.rows, :], self.slots.sent)

    for j in range(2):
        spots = pl.ds(pl.multiple_of(side * half + j * 128, 128), 128)
        weights[pl.ds(pl.multiple_of(spot * p_rows, 16), p_rows), spots] = par[
            pl.ds(2 * side + j, p_rows, stride=4), :
        ].astype(BF)
        land[side, pl.ds(pl.multiple_of(spot * b_rows, 16), b_rows), cols(j)] = bok[
            pl.ds(j, b_rows, stride=2), :
        ].astype(BF)
    slots_b, slots_p = Slots(), Slots()
    gather_b = Gather(b_view, None, slots_b)
    gather_p, gather_q = Gather(p_view, (0, 6), slots_p), Gather(p_view, (6, 16), slots_p)
    pl.semaphore_wait(barrier, len(near))
    gather_p.start()
    gather_b.start()
    loss[...] = jnp.zeros_like(loss)
    disc_t[...] = jnp.transpose(disc[...])
    score_col[...] = jnp.transpose(jnp.broadcast_to(score[...], (128, score.shape[1])))

    def fetch(clip):
        wave_copy(clip, clip % WAVES).wait()
        return waves.at[clip % WAVES]

    def free(clip):
        @pl.when(clip + WAVES < clip_count)
        def _():
            wave_copy(clip + WAVES, clip % WAVES).start()

    def both(*steps):
        def run():
            for step in steps:
                step()

        return run

    part = functools.partial
    early, late, every = (0,), (1, 2, 3), (0, 1, 2, 3)
    load_signal(
        clip_count, side, fetch, free, lens, codes, pad, ipad, crow, mask, sig,
        {7: both(part(gather_p.back, early), part(gather_b.back, early))},
    )
    real_side(
        (0, pairs), sig, disc_t, spec_t, feat_real, mag_real,
        {2: gather_p.step, 4: gather_b.step, 5: part(gather_p.back, late)},
    )
    gather_p.finish(every)
    gather_b.back(late)
    gather_p.settle()
    enc = weights.at[0:enc_rows, :]
    dec = weights.at[enc_rows : enc_rows + dec_rows, :]
    enc_t = dec_t.at[:, 0:enc_rows]
    enc_t[...] = jnp.transpose(enc[...])
    encode(
        (0, pairs), enc_t, sig, slope,
        {0: gather_q.start, 2: part(gather_b.finish, every), 5: part(gather_q.back, early)},
    )
    gather_b.settle()
    for group in range(2):
        books_t[group] = jnp.transpose(land[group])
    wait_sent(b_view(0, 15), slots_b.sent)
    pick(
        (0, pairs), crow, mask, books_t, quant, slope, loss,
        {1: gather_q.step, 3: part(gather_q.back, late), 5: part(gather_q.finish, every)},
    )

    d_dec = feat_real
    stage_b, got_b = land.at[0], land.at[1]
    scatter_b = Scatter(None, b_rows, acc_b, stage_b, got_b, (one_b, two_b, three_b), Slots())

    def far_books(level, carry):
        rows = pl.ds(pl.multiple_of(other * half, half), half)
        values = book_grad(clip_count, crow, slope, 2 * other + level, rows)
        stage_b[lanes(level, CB), :] = values.astype(BF)
        return carry

    def near_books(level, carry):
        rows = pl.ds(pl.multiple_of(side * half, half), half)
        acc_b[lanes(level, CB), :] = book_grad(clip_count, crow, slope, 2 * side + level, rows)
        return carry

    lax.fori_loop(0, 2, far_books, 0)
    gather_q.settle()
    scatter_b.pair.start()
    lax.fori_loop(0, 2, near_books, 0)
    wait_sent(p_view(0, 15), slots_p.sent)
    scatter_b.round_one()

    dec_t[...] = jnp.transpose(dec[...])
    for j in range(4):
        flat[pl.ds(j, out_rows, stride=4), :] = weights[
            enc_rows + dec_rows :, cols(j)
        ].astype(F32)
    unflatten_out(flat, square)
    edges = [(k, k * 128, min(k * 128 + 128, samples)) for k in range(3)]
    for k, start, stop in edges:
        out[:, start:stop] = square[k, :, 0 : stop - start].astype(BF)
    out_t[...] = jnp.transpose(out[...])
    decode_refs = (
        quant, dec_t, out, out_t, mask, sig, spec, spec_t, disc, disc_t, score_col,
        feat_real, mag_real, hidden, d_out, d_dec,
    )
    decode(
        (0, pairs), decode_refs, loss, {1: scatter_b.round_two, 3: scatter_b.round_three}
    )

    grad_out = dot_nt(hidden[...], d_out[...])
    for k, start, stop in edges:
        square[k, :, 0 : stop - start] = grad_out[:, start:stop]
    flatten_out(square, flat)
    low = enc_rows + dec_rows
    for j in range(2):
        near_part = flat[pl.ds(2 * side + j, out_rows, stride=4), :]
        far_part = flat[pl.ds(2 * other + j, out_rows, stride=4), :]
        acc_p[low : low + out_rows, cols(j)] = near_part
        stage_p[low : low + out_rows, cols(j)] = far_part.astype(BF)

    landed, slots = (one_p, two_p, three_p), Slots()
    scatter_d = Scatter((6, 16), p_rows, acc_p, stage_p, got_p, landed, slots)
    scatter_e = Scatter((0, 6), p_rows, acc_p, stage_p, got_p, landed, slots)
    near_rows = pl.ds(pl.multiple_of(side * half, half), half)
    far_rows = pl.ds(pl.multiple_of(other * half, half), half)
    for k, shift in ((1, None), (0, before), (2, after)):
        values = quant
        if shift is not None:
            values = hidden
            hidden[...] = shift(quant[...])
        rows = slice(enc_rows + k * width, enc_rows + (k + 1) * width)
        stage_p[rows, :] = dot_nt(values[...], d_dec[far_rows, :]).astype(BF)
        if k == 2:
            scatter_d.pair.start()
            scatter_b.settle()
            scatter_b.drain()
        acc_p[rows, :] = dot_nt(values[...], d_dec[near_rows, :])
    d_out[...] = before(sig[...])
    hidden[0:samples, :] = after(sig[...])
    shifted = (d_out, sig, hidden.at[0:samples, :])
    valid = jnp.sum(mask[...])
    lost = jnp.sum(loss[...])
    first_lane = lax.broadcasted_iota(jnp.int32, (8, 128), 1) == 0
    stat[0] = jnp.where(first_lane, lost, valid)
    swaps = [
        copy_to(device, stat.at[2 * k], stat.at[2 * k + 1], take("send"), take("recv"))
        for k, device in enumerate((pair_dev, first_dev, second_dev))
    ]
    level_sent, level_got = take("send"), take("recv")
    swaps[0].start()

    def stat_two():
        swaps[0].wait()
        stat[2] = stat[0] + stat[1]
        swaps[1].start()

    def stat_three():
        swaps[1].wait()
        stat[4] = stat[2] + stat[3]
        swaps[2].start()

    latent_back(
        (0, pairs), dec, d_dec, mask, slope, slope,
        {
            0: scatter_d.round_one,
            1: stat_two,
            3: stat_three,
            5: scatter_d.round_two,
        },
    )
    swaps[2].wait()
    zstat[z] = stat[4] + stat[5]
    for k in (1, 2, 3):
        copy_to(level_dev(around(k)), zstat.at[z], zstat.at[z], level_sent, level_got).start()
    for k, values in enumerate(shifted):
        rows = slice(k * samples, (k + 1) * samples)
        stage_p[rows, :] = dot_nt(values[...], slope[far_rows, :]).astype(BF)
    scatter_e.pair.start()
    for k, values in enumerate(shifted):
        rows = slice(k * samples, (k + 1) * samples)
        acc_p[rows, :] = dot_nt(values[...], slope[near_rows, :])
    scatter_e.round_one()
    scatter_d.round_three()
    wait_got(zstat.at[0:3], level_got)
    wait_sent(zstat.at[0:3], level_sent)
    totals[...] = (zstat[0] + zstat[1]) + (zstat[2] + zstat[3])
    own_b = pl.ds(pl.multiple_of(spot * b_rows, 16), b_rows)
    for j in range(2):
        grad_b[pl.ds(j, b_rows, stride=2), :] = acc_b[own_b, cols(j)]
    scatter_e.round_two()
    scatter_d.settle()
    scatter_e.round_three()
    scatter_e.settle()

    own_p = pl.ds(pl.multiple_of(spot * p_rows, 16), p_rows)
    swap = copy_to(pair_dev, acc_p.at[own_p, :], last, take("send"), take("recv"))
    swap.start()
    for j in range(2):
        grad_p[pl.ds(2 * side + j, p_rows, stride=4), :] = acc_p[own_p, cols(j)]
    scatter_e.drain()
    swap.wait()
    for j in range(2):
        grad_p[pl.ds(2 * other + j, p_rows, stride=4), :] = last[:, cols(j)]
    assert taken == {"send": SENDS, "recv": ARRIVALS}, taken


def fused(
    audio, lengths, codes, disc_weight, disc_score, params, params_mom, params_avg, books,
    books_mom, books_avg,
):
    clip_count, _, samples = audio.shape
    width = disc_weight.shape[1]
    half = width // 2
    chips = lax.axis_size("dp")
    total = clip_count * LANES
    table = spectral_table(samples)
    p_rows, b_rows = params.shape[0] // width, books.shape[1] // half
    all_rows, book_rows = p_rows * chips, b_rows * chips
    vmem = pl.BlockSpec(memory_space=pltpu.VMEM)
    smem = pl.BlockSpec(memory_space=pltpu.SMEM)
    p_shape = (params.shape[0] // 128, 128)
    b_shape = (books.shape[1] // 128, 128)
    all_clips = clip_count * chips * lax.axis_size("grp")
    weights = [value.reshape(p_shape) for value in (params, params_mom, params_avg)]
    tables = [value.reshape(b_shape) for value in (books, books_mom, books_avg)]
    grad_shapes = [jax.ShapeDtypeStruct(p_shape, F32), jax.ShapeDtypeStruct(b_shape, F32)]
    grads = pl.pallas_call(
        functools.partial(fused_kernel, 3 * samples, 3 * width),
        out_shape=grad_shapes + [jax.ShapeDtypeStruct((8, 128), F32)],
        in_specs=[pl.BlockSpec(memory_space=pl.ANY), smem] + [vmem] * 7,
        out_specs=[vmem] * 3,
        scratch_shapes=[
            pltpu.VMEM((samples, LANES), BF),
            pltpu.VMEM((8, LANES), jnp.int32),
            pltpu.VMEM((8, total), jnp.int32),
            pltpu.VMEM((1, total), F32),
            pltpu.VMEM((samples, total), BF),
            pltpu.VMEM((width, 3 * samples), BF),
            pltpu.VMEM((width, 128), F32),
            pltpu.VMEM((width, total), BF),
            pltpu.VMEM((samples // 2, total), F32),
            pltpu.VMEM((2, half, 2 * CB), BF),
            pltpu.VMEM((width, total), BF),
            pltpu.VMEM((width, total), BF),
            pltpu.VMEM((width, total), BF),
            pltpu.VMEM((width, 3 * width), BF),
            pltpu.VMEM((width, samples), BF),
            pltpu.VMEM((samples, width), BF),
            pltpu.VMEM((samples, total), BF),
            pltpu.VMEM((1, WIDE), F32),
            pltpu.VMEM((all_rows, width), BF),
            pltpu.VMEM((2, book_rows, half), BF),
            pltpu.VMEM((width * samples // 128, 128), F32),
            pltpu.VMEM((3, width, 128), F32),
            pltpu.VMEM((all_rows, half), F32),
            pltpu.VMEM((all_rows, half), BF),
            pltpu.VMEM((all_rows, half), BF),
            pltpu.VMEM((book_rows, half), F32),
            pltpu.VMEM((8, b_rows, half), BF),
            pltpu.VMEM((4, b_rows, half), BF),
            pltpu.VMEM((3, b_rows, half), BF),
            pltpu.VMEM((8, p_rows, half), BF),
            pltpu.VMEM((4, p_rows, half), BF),
            pltpu.VMEM((3, p_rows, half), BF),
            pltpu.VMEM((p_rows, half), F32),
            pltpu.VMEM((6, 8, 128), F32),
            pltpu.VMEM((4, 8, 128), F32),
            pltpu.VMEM((WAVES, samples, audio.shape[1]), BF),
            pltpu.SemaphoreType.DMA((SENDS,)),
            pltpu.SemaphoreType.DMA((ARRIVALS,)),
            pltpu.SemaphoreType.DMA((WAVES,)),
        ],
        compiler_params=pltpu.CompilerParams(
            vmem_limit_bytes=VMEM_LIMIT, collective_id=0, has_side_effects=True
        ),
        name="train_step",
    )(
        jnp.swapaxes(audio, 1, 2), lengths, codes, disc_weight, disc_score.reshape(1, width),
        jnp.asarray(table, BF), jnp.asarray(table.T, BF), weights[0], tables[0],
    )
    outs = pl.pallas_call(
        functools.partial(
            update_kernel, all_clips, 3 * samples * width // 128, 3 * width * width // 128
        ),
        out_shape=[grad_shapes[0]] * 3 + [grad_shapes[1]] * 3
        + [jax.ShapeDtypeStruct((1, 1), F32)] * 2,
        in_specs=[vmem] * 9,
        out_specs=[vmem] * 6 + [smem] * 2,
        name="train_update",
    )(*grads, *weights, *tables)
    return (
        *(value.reshape(params.shape) for value in outs[:3]),
        *(value.reshape(books.shape) for value in outs[3:6]),
        outs[6].reshape(()),
        outs[7].reshape(()),
    )


def solution(mesh):
    in_specs = (
        P(("dp", "grp"), None, None), P("dp"), P(None, None, "dp", None), P(), P(), P("dp"),
        P("dp"), P("dp"), P("grp", "dp"), P("grp", "dp"), P("grp", "dp"),
    )
    out_specs = (
        P("dp"), P("dp"), P("dp"), P("grp", "dp"), P("grp", "dp"), P("grp", "dp"), P(), P(),
    )
    body = fused if mesh.shape["dp"] == math.prod(CHIPS) else shards
    return jax.shard_map(body, mesh=mesh, in_specs=in_specs, out_specs=out_specs, check_vma=False)
```

```python
import functools
import math

import jax
import jax.numpy as jnp
import numpy as np
from jax import lax
from jax.experimental import pallas as pl
from jax.experimental.pallas import tpu as pltpu
from jax.sharding import PartitionSpec as P

BF = jnp.bfloat16
F32 = jnp.float32
MOMENTUM = 0.9
AVERAGE = 0.99
LANES = 256
CB = 1024
WIDE = 512
VMEM_LIMIT = 56 << 20


def spectral_table(samples):
    spots = np.arange(samples)[:, None]
    bins = np.arange(samples // 2)[None, :]
    turns = (spots * bins % samples) * (2.0 * math.pi / samples)
    window = 0.5 - 0.5 * np.cos((spots + 0.5) * (2.0 * math.pi / samples))
    table = np.concatenate([window * np.cos(turns), window * np.sin(turns)], axis=1)
    return (table * math.sqrt(2.0 / samples)).astype(np.float32)


def dot(left, right):
    return jnp.dot(left, right, preferred_element_type=F32)


def dot_nt(left, right):
    return lax.dot_general(left, right, (((1,), (1,)), ((), ())), preferred_element_type=F32)


def lanes(index, width):
    return pl.ds(pl.multiple_of(index * width, width), width)


def loop(bounds, step, hooks):
    hooks = dict(hooks)

    def body(index, carry):
        step(index)
        for after_index, hook in hooks.items():
            pl.when(index == after_index)(hook)
        return carry

    lax.fori_loop(*bounds, body, 0)


def col_sum(values):
    return jnp.sum(values, axis=0, keepdims=True)


def before(values):
    return pltpu.roll(values, 1, 1)


def after(values):
    return pltpu.roll(values, values.shape[1] - 1, 1)


def stack_three(values):
    return jnp.concatenate([before(values), values, after(values)], axis=0)


def silu_parts(values):
    sigmoid = 0.5 * jnp.tanh(0.5 * values) + 0.5
    return values * sigmoid, sigmoid * (1.0 + values * (1.0 - sigmoid))


def silu(values):
    return values * (0.5 * jnp.tanh(0.5 * values) + 0.5)


def load_signal(
    clip_count, side, fetch, free, lens, codes, pad, ipad, crow, mask, sig, hooks=()
):
    slots = codes.shape[3]
    pad[...] = jnp.zeros_like(pad)
    ipad[...] = jnp.full(ipad.shape, -1, jnp.int32)
    spots = lax.broadcasted_iota(jnp.int32, (1, LANES), 1)

    def step(clip):
        here = lanes(clip, LANES)
        row = side * clip_count + clip
        own = (spots < lens[row]).astype(F32)
        mask[:, here] = own
        for which in range(4):
            ipad[which : which + 1, 0:slots] = codes[which // 2, which % 2, pl.ds(row, 1), :]
        crow[:, here] = ipad[...]
        pad[:, 0:slots] = fetch(clip)[...]
        free(clip)
        wave = pad[...].astype(F32) * own
        sig[:, here] = wave.astype(BF)

    loop((0, clip_count), step, hooks)


def real_side(pairs, sig, disc_t, spec_t, feat_real, mag_real, hooks=()):
    samples = spec_t.shape[0]
    half = samples // 2

    def step(pair):
        here = lanes(pair, WIDE)
        wave = sig[:, here]
        feat_real[:, here] = silu(dot(disc_t[...], stack_three(wave))).astype(BF)
        spec = dot(spec_t[...], wave)
        norm = spec[:half] * spec[:half] + spec[half:] * spec[half:] + 1.0
        mag_real[:, here] = jnp.sqrt(norm)

    loop(pairs, step, hooks)


def onehot(crow, which, here, count):
    entries = lax.broadcasted_iota(jnp.int32, (CB, count), 0)
    return (entries == crow[pl.ds(which, 1), here]).astype(F32).astype(BF)


def encode(pairs, enc_t, sig, latent, hooks=()):
    def step(pair):
        here = lanes(pair, WIDE)
        latent[:, here] = dot(enc_t[...], stack_three(sig[:, here])).astype(BF)

    loop(pairs, step, hooks)


def pick(pairs, crow, mask, books_t, quant, slope, loss, hooks=()):
    half = books_t.shape[1]
    width = 2 * half

    def step(pair):
        here = lanes(pair, WIDE)
        own = mask[:, here]
        lost = jnp.zeros_like(own)
        for group in range(2):
            rows = slice(group * half, (group + 1) * half)
            hot = jnp.concatenate(
                [onehot(crow, 2 * group, here, WIDE), onehot(crow, 2 * group + 1, here, WIDE)], 0
            )
            value = dot(books_t[group], hot)
            quant[rows, here] = (value * own).astype(BF)
            gap = (slope[rows, here].astype(F32) - value) * own
            lost += col_sum(gap * gap)
            slope[rows, here] = (gap * (-2.0 / width)).astype(BF)
        loss[...] += lost * (1.0 / width)

    loop(pairs, step, hooks)


def book_grad(clip_count, crow, slope, which, rows):
    total = None
    chunk = 4 * LANES
    for part in range(clip_count * LANES // chunk):
        here = pl.ds(part * chunk, chunk)
        term = dot_nt(onehot(crow, which, here, chunk), slope[rows, here])
        total = term if total is None else total + term
    return total


def decode(pairs, refs, loss, hooks=()):
    (quant, dec_t, out, out_t, mask, sig, spec, spec_t, disc, disc_t, score_col) = refs[:11]
    (feat_real, mag_real, hidden, d_out, d_dec) = refs[11:]
    samples = spec.shape[0]
    width = hidden.shape[0]
    half = samples // 2

    def step(pair):
        here = lanes(pair, WIDE)
        own = mask[:, here]
        pre_dec = dot(dec_t[...], stack_three(quant[:, here]))
        act, act_slope = silu_parts(pre_dec)
        act = act.astype(BF)
        hidden[:, here] = act
        tanh_out = jnp.tanh(dot(out_t[...], act))
        made = tanh_out * own
        wave_gap = made - sig[:, here].astype(F32)
        norm = wave_gap * wave_gap + 1.0
        root = lax.rsqrt(norm)
        lost = col_sum(norm * root - 1.0) * (1.0 / samples)
        d_made = wave_gap * root * (1.0 / samples)
        made_low = made.astype(BF)

        spec_fake = dot(spec_t[...], made_low)
        real_part, imag_part = spec_fake[:half], spec_fake[half:]
        norm = real_part * real_part + imag_part * imag_part + 1.0
        root = lax.rsqrt(norm)
        spec_gap = norm * root - mag_real[:, here]
        norm = spec_gap * spec_gap + 1.0
        gap_root = lax.rsqrt(norm)
        lost += col_sum(norm * gap_root - 1.0) * (1.0 / samples)
        d_mag = spec_gap * gap_root * root * (1.0 / samples)
        d_spec = jnp.concatenate([d_mag * real_part, d_mag * imag_part], axis=0).astype(BF)
        d_made += dot(spec[...], d_spec)

        pre_fake = dot(disc_t[...], stack_three(made_low))
        feat_fake, feat_slope = silu_parts(pre_fake)
        weight = jnp.concatenate([score_col[...]] * (WIDE // 128), axis=1)
        miss = 1.0 - col_sum(feat_fake * weight)
        feat_gap = feat_fake - feat_real[:, here].astype(F32)
        norm = feat_gap * feat_gap + 1.0
        root = lax.rsqrt(norm)
        lost += own * (miss * miss + col_sum(norm * root - 1.0) * (1.0 / width))
        d_feat = (-2.0 * own * miss) * weight + (own * (1.0 / width)) * (feat_gap * root)
        d_fake = (d_feat * feat_slope).astype(BF)
        back = dot(disc[...], d_fake)
        d_made += after(back[:samples]) + back[samples : 2 * samples] + before(back[2 * samples :])

        d_pre_out = (d_made * own * (1.0 - tanh_out * tanh_out)).astype(BF)
        d_out[:, here] = d_pre_out
        d_dec[:, here] = (dot(out[...], d_pre_out) * act_slope).astype(BF)
        loss[...] += lost

    loop(pairs, step, hooks)


def latent_back(pairs, dec, d_dec, mask, slope, d_latent, hooks=()):
    width = d_dec.shape[0]

    def step(pair):
        here = lanes(pair, WIDE)
        back = dot(dec[...], d_dec[:, here])
        joined = after(back[:width]) + back[width : 2 * width] + before(back[2 * width :])
        joined = joined.astype(BF).astype(F32) * mask[:, here]
        d_latent[:, here] = (joined - slope[:, here].astype(F32)).astype(BF)

    loop(pairs, step, hooks)


def local_kernel(
    aud, lens, codes, disc, score, spec, spec_t, enc, dec, out, books,
    g_enc, g_dec, g_out, g_books, loss_out,
    pad, ipad, crow, mask, sig, disc_t, score_col, feat_real, mag_real,
    books_t, quant, hidden, enc_t, slope, dec_t, out_t, d_out, d_dec, loss,
):
    clip_count = aud.shape[0]
    pairs = (0, clip_count * LANES // WIDE)
    side = lax.axis_index("grp")
    loss[...] = jnp.zeros_like(loss)
    disc_t[...] = jnp.transpose(disc[...])
    score_col[...] = jnp.transpose(jnp.broadcast_to(score[...], (128, score.shape[1])))
    load_signal(
        clip_count, side, lambda clip: aud.at[clip], lambda clip: None, lens, codes, pad, ipad,
        crow, mask, sig,
    )
    real_side(pairs, sig, disc_t, spec_t, feat_real, mag_real)
    for group in range(2):
        books_t[group] = jnp.transpose(books[group])
    enc_t[...] = jnp.transpose(enc[...])
    dec_t[...] = jnp.transpose(dec[...])
    out_t[...] = jnp.transpose(out[...])
    encode(pairs, enc_t, sig, slope)
    pick(pairs, crow, mask, books_t, quant, slope, loss)

    def book_step(which, carry):
        rows = pl.ds(pl.multiple_of(which // 2 * 256, 256), 256)
        g_books[which] = book_grad(clip_count, crow, slope, which, rows)
        return carry

    lax.fori_loop(0, 4, book_step, 0)
    decode(
        pairs,
        (quant, dec_t, out, out_t, mask, sig, spec, spec_t, disc, disc_t, score_col,
         feat_real, mag_real, hidden, d_out, d_dec),
        loss,
    )
    g_out[...] = dot_nt(hidden[...], d_out[...])

    width = quant.shape[0]
    for part, shift in enumerate((before, lambda values: values, after)):
        g_dec[part * width : (part + 1) * width, :] = dot_nt(shift(quant[...]), d_dec[...])
    latent_back(pairs, dec, d_dec, mask, slope, hidden)

    samples = sig.shape[0]
    for part, shift in enumerate((before, lambda values: values, after)):
        g_enc[part * samples : (part + 1) * samples, :] = dot_nt(shift(sig[...]), hidden[...])
    loss_out[...] = loss[...]


def local_call(audio_t, lengths, codes, disc, score, enc, dec, out, books):
    clip_count, samples, _ = audio_t.shape
    width = disc.shape[1]
    total = clip_count * LANES
    table = spectral_table(samples)
    vmem = pl.BlockSpec(memory_space=pltpu.VMEM)
    smem = pl.BlockSpec(memory_space=pltpu.SMEM)
    return pl.pallas_call(
        local_kernel,
        out_shape=(
            jax.ShapeDtypeStruct((3 * samples, width), F32),
            jax.ShapeDtypeStruct((3 * width, width), F32),
            jax.ShapeDtypeStruct((width, samples), F32),
            jax.ShapeDtypeStruct((4, CB, width // 2), F32),
            jax.ShapeDtypeStruct((1, WIDE), F32),
        ),
        in_specs=[vmem, smem] + [vmem] * 9,
        out_specs=[vmem] * 5,
        scratch_shapes=[
            pltpu.VMEM((samples, LANES), BF),
            pltpu.VMEM((8, LANES), jnp.int32),
            pltpu.VMEM((8, total), jnp.int32),
            pltpu.VMEM((1, total), F32),
            pltpu.VMEM((samples, total), BF),
            pltpu.VMEM((width, 3 * samples), BF),
            pltpu.VMEM((width, 128), F32),
            pltpu.VMEM((width, total), BF),
            pltpu.VMEM((samples // 2, total), F32),
            pltpu.VMEM((2, width // 2, 2 * CB), BF),
            pltpu.VMEM((width, total), BF),
            pltpu.VMEM((width, total), BF),
            pltpu.VMEM((width, 3 * samples), BF),
            pltpu.VMEM((width, total), BF),
            pltpu.VMEM((width, 3 * width), BF),
            pltpu.VMEM((samples, width), BF),
            pltpu.VMEM((samples, total), BF),
            pltpu.VMEM((width, total), BF),
            pltpu.VMEM((1, WIDE), F32),
        ],
        compiler_params=pltpu.CompilerParams(vmem_limit_bytes=56 << 20),
        name="train_local",
    )(
        audio_t, lengths, codes, disc, score.reshape(1, width),
        jnp.asarray(table, BF), jnp.asarray(table.T, BF), enc, dec, out, books,
    )


def shards(
    audio, lengths, codes, disc_weight, disc_score, params, params_mom, params_avg, books,
    books_mom, books_avg,
):
    clip_count, slot_count, samples = audio.shape
    width = disc_weight.shape[1]
    half_width = width // 2
    side = lax.axis_index("grp")
    shared = lax.all_gather(params.astype(BF), "dp", axis=0, tiled=True)
    table = lax.all_gather(books.astype(BF), ("grp", "dp"), axis=1, tiled=True)
    enc_size = 3 * samples * width
    dec_size = 3 * width * width
    enc_weight = shared[:enc_size].reshape(3 * samples, width)
    dec_weight = shared[enc_size : enc_size + dec_size].reshape(3 * width, width)
    out_weight = shared[enc_size + dec_size :].reshape(width, samples)
    codebook = table.reshape(2, 2 * CB, half_width)
    local_count = jnp.sum(
        lax.dynamic_slice_in_dim(lengths, side * clip_count, clip_count, 0)
    ).astype(F32)
    frame_count = lax.psum(local_count, ("dp", "grp"))
    grad_enc, grad_dec, grad_out, grad_book, lost = local_call(
        jnp.swapaxes(audio, 1, 2), lengths, codes, disc_weight, disc_score,
        enc_weight, dec_weight, out_weight, codebook,
    )
    grad_shared = jnp.concatenate(
        [grad_enc.reshape(-1), grad_dec.reshape(-1), grad_out.reshape(-1)]
    )
    grad_shared = lax.psum(grad_shared.astype(BF), "grp").astype(F32)
    grad_book = lax.psum_scatter(
        grad_book.reshape(2, -1), "grp", scatter_dimension=0, tiled=True
    )
    shared_part = lax.psum_scatter(grad_shared, "dp", scatter_dimension=0, tiled=True)
    book_part = lax.psum_scatter(grad_book, "dp", scatter_dimension=1, tiled=True)
    loss_sum = lax.psum(jnp.sum(lost), ("dp", "grp"))
    all_clips = clip_count * lax.axis_size("dp") * lax.axis_size("grp")
    root = math.sqrt(131.0 * all_clips)
    shard_length = params.shape[0]
    spots = lax.axis_index("dp") * shard_length + jnp.arange(shard_length)
    rate = (
        jnp.where(spots < enc_size, 0.65, jnp.where(spots < enc_size + dec_size, 0.14, 0.2)) * root
    )
    shared_grad = shared_part / frame_count
    mom_new = MOMENTUM * params_mom + shared_grad
    param_new = params - rate * (shared_grad + MOMENTUM * mom_new)
    avg_new = AVERAGE * params_avg + (1.0 - AVERAGE) * param_new
    book_rate = 3.9 * math.sqrt(131.0 * all_clips * CB)
    book_grad_mean = book_part / frame_count
    book_mom_new = MOMENTUM * books_mom + book_grad_mean
    book_new = books - book_rate * (book_grad_mean + MOMENTUM * book_mom_new)
    book_avg_new = AVERAGE * books_avg + (1.0 - AVERAGE) * book_new
    return (
        param_new, mom_new, avg_new, book_new, book_mom_new, book_avg_new, loss_sum, frame_count,
    )


MESH = pl.DeviceIdType.MESH
ENC_RATE, DEC_RATE, OUT_RATE, BOOK_RATE = 0.65, 0.14, 0.2, 3.9
CHIPS = (4, 2, 2)
SENDS, ARRIVALS = 16, 72
WAVES = 4


def cols(index, width=128):
    return slice(index * width, (index + 1) * width)


def unflatten_out(flat, square):
    count = square.shape[1] // 2
    left = lax.broadcasted_iota(jnp.int32, (count, 128), 1) < 64
    part = [flat[pl.ds(k, count, stride=5), :] for k in range(5)]
    turned = [pltpu.roll(part[k], 64, 1) for k in (2, 3, 4)]
    even = part[:3]
    odd = [
        jnp.where(left, turned[0], turned[1]), jnp.where(left, turned[1], turned[2]), turned[2],
    ]
    for k in range(3):
        square[k, pl.ds(0, count, stride=2), :] = even[k]
        square[k, pl.ds(1, count, stride=2), :] = odd[k]


def flatten_out(square, flat):
    count = square.shape[1] // 2
    left = lax.broadcasted_iota(jnp.int32, (count, 128), 1) < 64
    even = [square[k, pl.ds(0, count, stride=2), :] for k in range(3)]
    odd = [square[k, pl.ds(1, count, stride=2), :] for k in range(3)]
    turned = [pltpu.roll(values, 64, 1) for values in odd]
    part = [
        even[0], even[1], jnp.where(left, even[2], turned[0]),
        jnp.where(left, turned[0], turned[1]), jnp.where(left, turned[1], turned[2]),
    ]
    for k in range(5):
        flat[pl.ds(k, count, stride=5), :] = part[k]


def update_kernel(
    all_clips, enc_chunks, dec_chunks, grad_p, grad_b, totals,
    par, pmom, pavg, bok, bmom, bavg,
    par_new, pmom_new, pavg_new, bok_new, bmom_new, bavg_new, loss, count,
):
    loss[0, 0] = totals[0, 0]
    count[0, 0] = totals[0, 1]
    frames = totals[0:1, 1:2]
    root = math.sqrt(131.0 * all_clips)
    where = lax.axis_index("dp") * par.shape[0] + lax.broadcasted_iota(jnp.int32, par.shape, 0)
    rate = root * jnp.where(
        where < enc_chunks, ENC_RATE,
        jnp.where(where < enc_chunks + dec_chunks, DEC_RATE, OUT_RATE),
    )

    def write(grad, rate, old, mom, avg, new_ref, mom_ref, avg_ref):
        grad = grad[...] / frames
        mom_new = MOMENTUM * mom[...] + grad
        new = old[...] - rate * (grad + MOMENTUM * mom_new)
        new_ref[...] = new
        mom_ref[...] = mom_new
        avg_ref[...] = AVERAGE * avg[...] + (1.0 - AVERAGE) * new

    write(grad_p, rate, par, pmom, pavg, par_new, pmom_new, pavg_new)
    write(grad_b, BOOK_RATE * root * math.sqrt(CB), bok, bmom, bavg, bok_new, bmom_new, bavg_new)


def fused_kernel(
    enc_rows, dec_rows,
    aud, lens, codes, disc, score, spec, spec_t, par, bok, grad_p, grad_b, totals,
    pad, ipad, crow, mask, sig, disc_t, score_col, feat_real, mag_real,
    books_t, quant, hidden, slope, dec_t, out, out_t, d_out, loss,
    weights, land, flat, square, acc_p, stage_p, got_p, acc_b,
    one_b, two_b, three_b, one_p, two_p, three_p,
    last, stat, zstat, waves, send, recv, wave_sem,
):
    clip_count = aud.shape[0]
    width, samples = disc_t.shape[0], sig.shape[0]
    half = width // 2
    pairs = clip_count * LANES // WIDE
    spot = lax.axis_index("dp")
    side = lax.axis_index("grp")
    other = 1 - side
    p_rows = par.shape[0] * 128 // width
    b_rows = bok.shape[0] * 128 // half
    out_rows = weights.shape[0] - enc_rows - dec_rows

    z, y, x = spot // 4, spot // 2 % 2, spot % 2
    mine_first = y + side * (x - y)
    mine_second = x + side * (y - x)

    def unit(level, first, second):
        return 4 * level + (2 - side) * first + (1 + side) * second

    def around(step):
        return (z + step) % 4

    first_dev = (unit(z, 1 - mine_first, mine_second), side)
    second_dev = (unit(z, mine_first, 1 - mine_second), side)
    pair_dev = (spot, other)

    def level_dev(level):
        return (unit(level, mine_first, mine_second), side)

    barrier = pltpu.get_barrier_semaphore()
    near = [first_dev, second_dev, pair_dev] + [level_dev(around(k)) for k in (1, 2, 3)]
    for device in near:
        pl.semaphore_signal(barrier, inc=1, device_id=device, device_id_type=MESH)

    def wave_copy(clip, slot):
        return pltpu.make_async_copy(aud.at[clip], waves.at[slot], wave_sem.at[slot])

    for slot in range(WAVES):
        wave_copy(slot, slot).start()
    taken = {"send": 0, "recv": 0}

    def take(kind, count=1):
        taken[kind] += count
        return taken[kind] - count

    def copy_to(device, src, dst, send_at, recv_at):
        return pltpu.make_async_remote_copy(
            src_ref=src, dst_ref=dst, send_sem=send.at[send_at], recv_sem=recv.at[recv_at],
            device_id=device, device_id_type=MESH,
        )

    def block(ref, rows, which):
        return ref.at[pl.ds(pl.multiple_of(which * rows, 16), rows), :]

    def p_view(which, count=1):
        rows = pl.ds(pl.multiple_of(which * p_rows, 16), count * p_rows)
        return weights.at[rows, lanes(side, half)]

    def b_view(which, count=1):
        rows = pl.ds(pl.multiple_of(which * b_rows, 16), count * b_rows)
        return land.at[side, rows, :]

    def held(span, which, run):
        if span is None:
            run()
        else:
            pl.when((which >= span[0]) & (which < span[1]))(run)

    def wait_sent(ref, at):
        copy_to(pair_dev, ref, ref, at, 0).wait_send()

    def wait_got(ref, at):
        copy_to(pair_dev, ref, ref, 0, at).wait_recv()

    class Slots:
        def __init__(self):
            self.sent = take("send")
            self.got = take("recv", 15)

    class Gather:
        def __init__(self, view, span, slots):
            self.view, self.span, self.slots = view, span, slots
            self.swap_sent, self.swap_got = take("send"), take("recv")

            def make(slot, which, device):
                return copy_to(
                    device, view(which), view(which), slots.sent, slots.got + slot
                )

            self.levels, self.firsts, self.seconds = [], [], []
            for k in range(4):
                here = unit(around(4 - k), mine_first, mine_second)
                there = unit(around(4 - k), 1 - mine_first, mine_second)
                if k:
                    self.levels.append(make(k - 1, spot, level_dev(around(k))))
                self.firsts.append(make(3 + k, here, first_dev))
                self.seconds.append(
                    [make(7 + 2 * k, here, second_dev), make(8 + 2 * k, there, second_dev)]
                )

        def swap(self, which):
            copy_to(
                pair_dev, self.view(which), self.view(which), self.swap_sent, self.swap_got
            ).start()

        def start(self):
            def run():
                for copy in self.levels + [self.firsts[0], self.seconds[0][0]]:
                    copy.start()
                self.swap(spot)

            held(self.span, spot, run)

        def step(self):
            for k in (1, 2, 3):
                which = unit(around(4 - k), mine_first, mine_second)

                def run(k=k, which=which):
                    self.levels[k - 1].wait_recv()
                    self.firsts[k].start()
                    self.seconds[k][0].start()
                    self.swap(which)

                held(self.span, which, run)

        def back(self, ks):
            for k in ks:
                which = unit(around(4 - k), 1 - mine_first, mine_second)

                def run(k=k, which=which):
                    self.firsts[k].wait_recv()
                    self.seconds[k][1].start()
                    self.swap(which)

                held(self.span, which, run)

        def finish(self, ks):
            for k in ks:
                for slot, first in enumerate((mine_first, 1 - mine_first)):
                    which = unit(around(4 - k), first, 1 - mine_second)

                    def run(k=k, slot=slot, which=which):
                        self.seconds[k][slot].wait_recv()
                        self.swap(which)

                    held(self.span, which, run)

        def settle(self):
            wait_got(self.view(*self.span_units()), self.swap_got)
            wait_sent(self.view(*self.span_units()), self.swap_sent)

        def span_units(self):
            start, stop = self.span or (0, 16)
            return start, stop - start

    class Scatter:
        def __init__(self, span, rows, acc, stage, got, landed, slots):
            self.span, self.rows, self.acc, self.stage, self.got = span, rows, acc, stage, got
            self.landed, self.slots = landed, slots
            start, stop = span or (0, 16)
            self.levels = list(range(start // 4, (stop + 3) // 4))
            both_rows = pl.ds(start * rows, (stop - start) * rows)
            self.pair = copy_to(
                pair_dev, stage.at[both_rows, :], got.at[both_rows, :], take("send"), take("recv")
            )
            one, two, three = landed
            self.sent_one, self.kept_one, self.sent_two, self.kept_two = [], [], [], []
            for level in self.levels:
                for first in range(2):
                    slot = 2 * level + first
                    which = unit(level, first, 1 - mine_second)
                    self.sent_one.append((which, copy_to(
                        second_dev, block(stage, rows, which), one.at[slot],
                        slots.sent, slots.got + slot,
                    )))
                    self.kept_one.append((unit(level, first, mine_second), one, slot))
                which = unit(level, 1 - mine_first, mine_second)
                self.sent_two.append((which, copy_to(
                    first_dev, block(stage, rows, which), two.at[level],
                    slots.sent, slots.got + 8 + level,
                )))
                self.kept_two.append((unit(level, mine_first, mine_second), two, level))

        def read(self, ref, which):
            return ref[pl.ds(pl.multiple_of(which * self.rows, 16), self.rows), :]

        def put(self, ref, which, values):
            ref[pl.ds(pl.multiple_of(which * self.rows, 16), self.rows), :] = values

        def round_one(self):
            self.pair.wait()
            for which, copy in self.sent_one:
                def run(which=which, copy=copy):
                    total = self.read(self.acc, which) + self.read(self.got, which).astype(F32)
                    self.put(self.stage, which, total.astype(BF))
                    copy.start()

                held(self.span, which, run)
            for which, _, _ in self.kept_one:
                def keep(which=which):
                    total = self.read(self.acc, which) + self.read(self.got, which).astype(F32)
                    self.put(self.acc, which, total)

                held(self.span, which, keep)

        def fold(self, kept, sent):
            for (which, landed, slot), (_, copy) in zip(kept, sent):
                def run(which=which, landed=landed, slot=slot, copy=copy):
                    copy.wait_recv()
                    self.put(
                        self.acc, which, self.read(self.acc, which) + landed[slot].astype(F32)
                    )

                held(self.span, which, run)

        def round_two(self):
            self.fold(self.kept_one, self.sent_one)
            for which, copy in self.sent_two:
                def run(which=which, copy=copy):
                    self.put(self.stage, which, self.read(self.acc, which).astype(BF))
                    copy.start()

                held(self.span, which, run)

        def round_three(self):
            self.fold(self.kept_two, self.sent_two)
            for level in self.levels:
                which = unit(level, mine_first, mine_second)
                slot = (z + 7 - level) % 4 % 3

                def run(level=level, which=which, slot=slot):
                    self.put(self.stage, which, self.read(self.acc, which).astype(BF))
                    copy_to(
                        level_dev(level), block(self.stage, self.rows, which),
                        self.landed[2].at[slot], self.slots.sent, self.slots.got + 12 + slot,
                    ).start()

                pl.when(z != level)(functools.partial(held, self.span, which, run))

        def settle(self):
            def run():
                total = self.read(self.acc, spot)
                for slot in range(3):
                    wait_got(self.landed[2].at[slot], self.slots.got + 12 + slot)
                    total = total + self.landed[2][slot].astype(F32)
                self.put(self.acc, spot, total)

            held(self.span, spot, run)

        def drain(self):
            wait_sent(self.stage.at[0 : 15 * self.rows, :], self.slots.sent)

    for j in range(2):
        spots = pl.ds(pl.multiple_of(side * half + j * 128, 128), 128)
        weights[pl.ds(pl.multiple_of(spot * p_rows, 16), p_rows), spots] = par[
            pl.ds(2 * side + j, p_rows, stride=4), :
        ].astype(BF)
        land[side, pl.ds(pl.multiple_of(spot * b_rows, 16), b_rows), cols(j)] = bok[
            pl.ds(j, b_rows, stride=2), :
        ].astype(BF)
    slots_b, slots_p = Slots(), Slots()
    gather_b = Gather(b_view, None, slots_b)
    gather_p, gather_q = Gather(p_view, (0, 6), slots_p), Gather(p_view, (6, 16), slots_p)
    pl.semaphore_wait(barrier, len(near))
    gather_p.start()
    gather_b.start()
    gather_q.start()
    loss[...] = jnp.zeros_like(loss)
    disc_t[...] = jnp.transpose(disc[...])
    score_col[...] = jnp.transpose(jnp.broadcast_to(score[...], (128, score.shape[1])))

    def fetch(clip):
        wave_copy(clip, clip % WAVES).wait()
        return waves.at[clip % WAVES]

    def free(clip):
        @pl.when(clip + WAVES < clip_count)
        def _():
            wave_copy(clip + WAVES, clip % WAVES).start()

    def both(*steps):
        def run():
            for step in steps:
                step()

        return run

    part = functools.partial
    early, late, every = (0,), (1, 2, 3), (0, 1, 2, 3)
    load_signal(
        clip_count, side, fetch, free, lens, codes, pad, ipad, crow, mask, sig,
        {7: both(part(gather_p.back, early), part(gather_b.back, early), part(gather_q.back, early))},
    )
    real_side(
        (0, pairs), sig, disc_t, spec_t, feat_real, mag_real,
        {3: gather_p.step, 4: gather_b.step, 5: part(gather_p.back, late)},
    )
    gather_q.step()
    gather_b.back(late)
    gather_p.finish(every)
    gather_p.settle()
    enc = weights.at[0:enc_rows, :]
    dec = weights.at[enc_rows : enc_rows + dec_rows, :]
    enc_t = dec_t.at[:, 0:enc_rows]
    enc_t[...] = jnp.transpose(enc[...])
    encode(
        (0, pairs), enc_t, sig, slope,
        {0: part(gather_q.back, late), 2: part(gather_b.finish, every)},
    )
    gather_b.settle()
    for group in range(2):
        books_t[group] = jnp.transpose(land[group])
    wait_sent(b_view(0, 15), slots_b.sent)
    pick(
        (0, pairs), crow, mask, books_t, quant, slope, loss,
        {0: part(gather_q.finish, every)},
    )

    d_dec = feat_real
    stage_b, got_b = land.at[0], land.at[1]
    scatter_b = Scatter(None, b_rows, acc_b, stage_b, got_b, (one_b, two_b, three_b), Slots())

    def far_books(level, carry):
        rows = pl.ds(pl.multiple_of(other * half, half), half)
        values = book_grad(clip_count, crow, slope, 2 * other + level, rows)
        stage_b[lanes(level, CB), :] = values.astype(BF)
        return carry

    def near_books(level, carry):
        rows = pl.ds(pl.multiple_of(side * half, half), half)
        acc_b[lanes(level, CB), :] = book_grad(clip_count, crow, slope, 2 * side + level, rows)
        return carry

    lax.fori_loop(0, 2, far_books, 0)
    gather_q.settle()
    scatter_b.pair.start()
    lax.fori_loop(0, 2, near_books, 0)
    wait_sent(p_view(0, 15), slots_p.sent)
    scatter_b.round_one()

    dec_t[...] = jnp.transpose(dec[...])
    for j in range(4):
        flat[pl.ds(j, out_rows, stride=4), :] = weights[
            enc_rows + dec_rows :, cols(j)
        ].astype(F32)
    unflatten_out(flat, square)
    edges = [(k, k * 128, min(k * 128 + 128, samples)) for k in range(3)]
    for k, start, stop in edges:
        out[:, start:stop] = square[k, :, 0 : stop - start].astype(BF)
    out_t[...] = jnp.transpose(out[...])
    decode_refs = (
        quant, dec_t, out, out_t, mask, sig, spec, spec_t, disc, disc_t, score_col,
        feat_real, mag_real, hidden, d_out, d_dec,
    )
    decode(
        (0, pairs), decode_refs, loss, {1: scatter_b.round_two, 3: scatter_b.round_three}
    )

    far_rows = pl.ds(pl.multiple_of(other * half, half), half)
    near_rows = pl.ds(pl.multiple_of(side * half, half), half)
    turned = dec_t

    def shifted_grads(values, low, grad):
        count, span = values.shape[0], turned.shape[1]
        for k, shift in enumerate((before, None, after)):
            far, near = 0.0, 0.0
            for start in range(0, values.shape[1], span):
                here = slice(start, start + span)
                left = values.at[:, here]
                if shift is not None:
                    left = turned.at[0:count, :]
                    left[...] = shift(values[:, here])
                far += dot_nt(left[...], grad[far_rows, here])
                near += dot_nt(left[...], grad[near_rows, here])
            rows = slice(low + k * count, low + (k + 1) * count)
            stage_p[rows, :] = far.astype(BF)
            acc_p[rows, :] = near

    landed, slots = (one_p, two_p, three_p), Slots()
    scatter_d = Scatter((6, 14), p_rows, acc_p, stage_p, got_p, landed, slots)
    scatter_e = Scatter((0, 6), p_rows, acc_p, stage_p, got_p, landed, slots)
    scatter_o = Scatter((14, 16), p_rows, acc_p, stage_p, got_p, landed, slots)
    shifted_grads(quant, enc_rows, d_dec)
    scatter_d.pair.start()
    scatter_b.settle()
    scatter_b.drain()

    valid = jnp.sum(mask[...])
    lost = jnp.sum(loss[...])
    first_lane = lax.broadcasted_iota(jnp.int32, (8, 128), 1) == 0
    stat[0] = jnp.where(first_lane, lost, valid)
    swaps = [
        copy_to(device, stat.at[2 * k], stat.at[2 * k + 1], take("send"), take("recv"))
        for k, device in enumerate((pair_dev, first_dev, second_dev))
    ]
    level_sent, level_got = take("send"), take("recv")
    swaps[0].start()

    def stat_two():
        swaps[0].wait()
        stat[2] = stat[0] + stat[1]
        swaps[1].start()

    def stat_three():
        swaps[1].wait()
        stat[4] = stat[2] + stat[3]
        swaps[2].start()

    latent_back(
        (0, pairs), dec, d_dec, mask, slope, slope,
        {
            0: scatter_d.round_one,
            1: stat_two,
            3: stat_three,
            5: scatter_d.round_two,
        },
    )
    swaps[2].wait()
    zstat[z] = stat[4] + stat[5]
    for k in (1, 2, 3):
        copy_to(level_dev(around(k)), zstat.at[z], zstat.at[z], level_sent, level_got).start()
    shifted_grads(sig, 0, slope)
    scatter_e.pair.start()
    grad_out = dot_nt(hidden[...], d_out[...])
    for k, start, stop in edges:
        square[k, :, 0 : stop - start] = grad_out[:, start:stop]
    scatter_e.round_one()
    flatten_out(square, flat)
    low = enc_rows + dec_rows
    for j in range(2):
        near_part = flat[pl.ds(2 * side + j, out_rows, stride=4), :]
        far_part = flat[pl.ds(2 * other + j, out_rows, stride=4), :]
        acc_p[low : low + out_rows, cols(j)] = near_part
        stage_p[low : low + out_rows, cols(j)] = far_part.astype(BF)
    scatter_o.pair.start()
    scatter_d.round_three()
    wait_got(zstat.at[0:3], level_got)
    wait_sent(zstat.at[0:3], level_sent)
    totals[...] = (zstat[0] + zstat[1]) + (zstat[2] + zstat[3])
    own_b = pl.ds(pl.multiple_of(spot * b_rows, 16), b_rows)
    for j in range(2):
        grad_b[pl.ds(j, b_rows, stride=2), :] = acc_b[own_b, cols(j)]
    scatter_e.round_two()
    scatter_o.round_one()
    scatter_d.settle()
    scatter_e.round_three()
    scatter_o.round_two()
    scatter_e.settle()
    scatter_o.round_three()
    scatter_o.settle()

    own_p = pl.ds(pl.multiple_of(spot * p_rows, 16), p_rows)
    swap = copy_to(pair_dev, acc_p.at[own_p, :], last, take("send"), take("recv"))
    swap.start()
    for j in range(2):
        grad_p[pl.ds(2 * side + j, p_rows, stride=4), :] = acc_p[own_p, cols(j)]
    scatter_e.drain()
    swap.wait()
    for j in range(2):
        grad_p[pl.ds(2 * other + j, p_rows, stride=4), :] = last[:, cols(j)]
    assert taken == {"send": SENDS, "recv": ARRIVALS}, taken


def fused(
    audio, lengths, codes, disc_weight, disc_score, params, params_mom, params_avg, books,
    books_mom, books_avg,
):
    clip_count, _, samples = audio.shape
    width = disc_weight.shape[1]
    half = width // 2
    chips = lax.axis_size("dp")
    total = clip_count * LANES
    table = spectral_table(samples)
    p_rows, b_rows = params.shape[0] // width, books.shape[1] // half
    all_rows, book_rows = p_rows * chips, b_rows * chips
    vmem = pl.BlockSpec(memory_space=pltpu.VMEM)
    smem = pl.BlockSpec(memory_space=pltpu.SMEM)
    p_shape = (params.shape[0] // 128, 128)
    b_shape = (books.shape[1] // 128, 128)
    all_clips = clip_count * chips * lax.axis_size("grp")
    weights = [value.reshape(p_shape) for value in (params, params_mom, params_avg)]
    tables = [value.reshape(b_shape) for value in (books, books_mom, books_avg)]
    grad_shapes = [jax.ShapeDtypeStruct(p_shape, F32), jax.ShapeDtypeStruct(b_shape, F32)]
    grads = pl.pallas_call(
        functools.partial(fused_kernel, 3 * samples, 3 * width),
        out_shape=grad_shapes + [jax.ShapeDtypeStruct((8, 128), F32)],
        in_specs=[pl.BlockSpec(memory_space=pl.ANY), smem] + [vmem] * 7,
        out_specs=[vmem] * 3,
        scratch_shapes=[
            pltpu.VMEM((samples, LANES), BF),
            pltpu.VMEM((8, LANES), jnp.int32),
            pltpu.VMEM((8, total), jnp.int32),
            pltpu.VMEM((1, total), F32),
            pltpu.VMEM((samples, total), BF),
            pltpu.VMEM((width, 3 * samples), BF),
            pltpu.VMEM((width, 128), F32),
            pltpu.VMEM((width, total), BF),
            pltpu.VMEM((samples // 2, total), F32),
            pltpu.VMEM((2, half, 2 * CB), BF),
            pltpu.VMEM((width, total), BF),
            pltpu.VMEM((width, total), BF),
            pltpu.VMEM((width, total), BF),
            pltpu.VMEM((width, 3 * width), BF),
            pltpu.VMEM((width, samples), BF),
            pltpu.VMEM((samples, width), BF),
            pltpu.VMEM((samples, total), BF),
            pltpu.VMEM((1, WIDE), F32),
            pltpu.VMEM((all_rows, width), BF),
            pltpu.VMEM((2, book_rows, half), BF),
            pltpu.VMEM((width * samples // 128, 128), F32),
            pltpu.VMEM((3, width, 128), F32),
            pltpu.VMEM((all_rows, half), F32),
            pltpu.VMEM((all_rows, half), BF),
            pltpu.VMEM((all_rows, half), BF),
            pltpu.VMEM((book_rows, half), F32),
            pltpu.VMEM((8, b_rows, half), BF),
            pltpu.VMEM((4, b_rows, half), BF),
            pltpu.VMEM((3, b_rows, half), BF),
            pltpu.VMEM((8, p_rows, half), BF),
            pltpu.VMEM((4, p_rows, half), BF),
            pltpu.VMEM((3, p_rows, half), BF),
            pltpu.VMEM((p_rows, half), F32),
            pltpu.VMEM((6, 8, 128), F32),
            pltpu.VMEM((4, 8, 128), F32),
            pltpu.VMEM((WAVES, samples, audio.shape[1]), BF),
            pltpu.SemaphoreType.DMA((SENDS,)),
            pltpu.SemaphoreType.DMA((ARRIVALS,)),
            pltpu.SemaphoreType.DMA((WAVES,)),
        ],
        compiler_params=pltpu.CompilerParams(
            vmem_limit_bytes=VMEM_LIMIT, collective_id=0, has_side_effects=True
        ),
        name="train_step",
    )(
        jnp.swapaxes(audio, 1, 2), lengths, codes, disc_weight, disc_score.reshape(1, width),
        jnp.asarray(table, BF), jnp.asarray(table.T, BF), weights[0], tables[0],
    )
    outs = pl.pallas_call(
        functools.partial(
            update_kernel, all_clips, 3 * samples * width // 128, 3 * width * width // 128
        ),
        out_shape=[grad_shapes[0]] * 3 + [grad_shapes[1]] * 3
        + [jax.ShapeDtypeStruct((1, 1), F32)] * 2,
        in_specs=[vmem] * 9,
        out_specs=[vmem] * 6 + [smem] * 2,
        name="train_update",
    )(*grads, *weights, *tables)
    return (
        *(value.reshape(params.shape) for value in outs[:3]),
        *(value.reshape(books.shape) for value in outs[3:6]),
        outs[6].reshape(()),
        outs[7].reshape(()),
    )


def solution(mesh):
    in_specs = (
        P(("dp", "grp"), None, None), P("dp"), P(None, None, "dp", None), P(), P(), P("dp"),
        P("dp"), P("dp"), P("grp", "dp"), P("grp", "dp"), P("grp", "dp"),
    )
    out_specs = (
        P("dp"), P("dp"), P("dp"), P("grp", "dp"), P("grp", "dp"), P("grp", "dp"), P(), P(),
    )
    body = fused if mesh.shape["dp"] == math.prod(CHIPS) else shards
    return jax.shard_map(body, mesh=mesh, in_specs=in_specs, out_specs=out_specs, check_vma=False)
```

```python
import functools
import math

import jax
import jax.numpy as jnp
import numpy as np
from jax import lax
from jax.experimental import pallas as pl
from jax.experimental.pallas import tpu as pltpu
from jax.sharding import PartitionSpec as P

BF = jnp.bfloat16
F32 = jnp.float32
MOMENTUM = 0.9
AVERAGE = 0.99
LANES = 256
CB = 1024
WIDE = 512
VMEM_LIMIT = 56 << 20


def spectral_table(samples):
    spots = np.arange(samples)[:, None]
    bins = np.arange(samples // 2)[None, :]
    turns = (spots * bins % samples) * (2.0 * math.pi / samples)
    window = 0.5 - 0.5 * np.cos((spots + 0.5) * (2.0 * math.pi / samples))
    table = np.concatenate([window * np.cos(turns), window * np.sin(turns)], axis=1)
    return (table * math.sqrt(2.0 / samples)).astype(np.float32)


def dot(left, right):
    return jnp.dot(left, right, preferred_element_type=F32)


def dot_nt(left, right):
    return lax.dot_general(left, right, (((1,), (1,)), ((), ())), preferred_element_type=F32)


def lanes(index, width):
    return pl.ds(pl.multiple_of(index * width, width), width)


def loop(bounds, step, hooks, per=1):
    hooks = dict(hooks)

    def body(index, carry):
        turns = [step(index * per + k) for k in range(per)]
        turns = [turn for turn in turns if turn is not None]
        while turns:
            turns = [turn for turn in turns if next(turn, turns) is not turns]
        for after_index, hook in hooks.items():
            pl.when(index == after_index // per)(hook)
        return carry

    lax.fori_loop(bounds[0] // per, bounds[1] // per, body, 0)


def col_sum(values):
    return jnp.sum(values, axis=0, keepdims=True)


def before(values):
    return pltpu.roll(values, 1, 1)


def after(values):
    return pltpu.roll(values, values.shape[1] - 1, 1)


def stack_three(values):
    return jnp.concatenate([before(values), values, after(values)], axis=0)


def silu_parts(values):
    sigmoid = 0.5 * jnp.tanh(0.5 * values) + 0.5
    return values * sigmoid, sigmoid * (1.0 + values * (1.0 - sigmoid))


def silu(values):
    return values * (0.5 * jnp.tanh(0.5 * values) + 0.5)


def load_signal(
    clip_count, side, fetch, free, lens, codes, pad, ipad, crow, mask, sig, hooks=()
):
    slots = codes.shape[3]
    pad[...] = jnp.zeros_like(pad)
    ipad[...] = jnp.full(ipad.shape, -1, jnp.int32)
    spots = lax.broadcasted_iota(jnp.int32, (1, LANES), 1)

    def step(clip):
        here = lanes(clip, LANES)
        row = side * clip_count + clip
        own = (spots < lens[row]).astype(F32)
        mask[:, here] = own
        for which in range(4):
            ipad[which : which + 1, 0:slots] = codes[which // 2, which % 2, pl.ds(row, 1), :]
        crow[:, here] = ipad[...]
        pad[:, 0:slots] = fetch(clip)[...]
        free(clip)
        wave = pad[...].astype(F32) * own
        sig[:, here] = wave.astype(BF)

    loop((0, clip_count), step, hooks)


def real_side(pairs, sig, disc_t, spec_t, feat_real, mag_real, hooks=()):
    samples = spec_t.shape[0]
    half = samples // 2

    def step(pair):
        here = lanes(pair, WIDE)
        wave = sig[:, here]
        feat_real[:, here] = silu(dot(disc_t[...], stack_three(wave))).astype(BF)
        spec = dot(spec_t[...], wave)
        norm = spec[:half] * spec[:half] + spec[half:] * spec[half:] + 1.0
        mag_real[:, here] = jnp.sqrt(norm)

    loop(pairs, step, hooks)


def onehot(crow, which, here, count):
    entries = lax.broadcasted_iota(jnp.int32, (CB, count), 0)
    return (entries == crow[pl.ds(which, 1), here]).astype(F32).astype(BF)


def encode(pairs, enc_t, sig, latent, hooks=()):
    def step(pair):
        here = lanes(pair, WIDE)
        latent[:, here] = dot(enc_t[...], stack_three(sig[:, here])).astype(BF)

    loop(pairs, step, hooks, 2)


def pick(pairs, crow, mask, books_t, quant, slope, loss, hooks=()):
    half = books_t.shape[1]
    width = 2 * half

    def step(pair):
        here = lanes(pair, WIDE)
        own = mask[:, here]
        lost = jnp.zeros_like(own)
        for group in range(2):
            rows = slice(group * half, (group + 1) * half)
            hot = jnp.concatenate(
                [onehot(crow, 2 * group, here, WIDE), onehot(crow, 2 * group + 1, here, WIDE)], 0
            )
            value = dot(books_t[group], hot)
            quant[rows, here] = (value * own).astype(BF)
            gap = (slope[rows, here].astype(F32) - value) * own
            lost += col_sum(gap * gap)
            slope[rows, here] = (gap * (-2.0 / width)).astype(BF)
        loss[...] += lost * (1.0 / width)

    loop(pairs, step, hooks, 2)


def book_grad(clip_count, crow, slope, which, rows):
    total = None
    chunk = 4 * LANES
    for part in range(clip_count * LANES // chunk):
        here = pl.ds(part * chunk, chunk)
        term = dot_nt(onehot(crow, which, here, chunk), slope[rows, here])
        total = term if total is None else total + term
    return total


def decode(pairs, refs, loss, hooks=(), per=1):
    (quant, dec_t, out, out_t, mask, sig, spec, spec_t, disc, disc_t, score_col) = refs[:11]
    (feat_real, mag_real, hidden, d_out, d_dec) = refs[11:]
    samples = spec.shape[0]
    width = hidden.shape[0]
    half = samples // 2

    def step(pair):
        here = lanes(pair, LANES)
        own = mask[:, here]
        pre_dec = dot(dec_t[...], stack_three(quant[:, here]))
        act, act_slope = silu_parts(pre_dec)
        act = act.astype(BF)
        yield
        hidden[:, here] = act
        tanh_out = jnp.tanh(dot(out_t[...], act))
        made = tanh_out * own
        yield
        wave_gap = made - sig[:, here].astype(F32)
        norm = wave_gap * wave_gap + 1.0
        root = lax.rsqrt(norm)
        lost = col_sum(norm * root - 1.0) * (1.0 / samples)
        d_made = wave_gap * root * (1.0 / samples)
        made_low = made.astype(BF)

        spec_fake = dot(spec_t[...], made_low)
        yield
        real_part, imag_part = spec_fake[:half], spec_fake[half:]
        norm = real_part * real_part + imag_part * imag_part + 1.0
        root = lax.rsqrt(norm)
        spec_gap = norm * root - mag_real[:, here]
        norm = spec_gap * spec_gap + 1.0
        gap_root = lax.rsqrt(norm)
        lost += col_sum(norm * gap_root - 1.0) * (1.0 / samples)
        d_mag = spec_gap * gap_root * root * (1.0 / samples)
        d_spec = jnp.concatenate([d_mag * real_part, d_mag * imag_part], axis=0).astype(BF)
        yield
        d_made += dot(spec[...], d_spec)

        pre_fake = dot(disc_t[...], stack_three(made_low))
        yield
        feat_fake, feat_slope = silu_parts(pre_fake)
        weight = jnp.concatenate([score_col[...]] * (LANES // 128), axis=1)
        miss = 1.0 - col_sum(feat_fake * weight)
        feat_gap = feat_fake - feat_real[:, here].astype(F32)
        norm = feat_gap * feat_gap + 1.0
        root = lax.rsqrt(norm)
        lost += own * (miss * miss + col_sum(norm * root - 1.0) * (1.0 / width))
        d_feat = (-2.0 * own * miss) * weight + (own * (1.0 / width)) * (feat_gap * root)
        d_fake = (d_feat * feat_slope).astype(BF)
        yield
        back = dot(disc[...], d_fake)
        d_made += after(back[:samples]) + back[samples : 2 * samples] + before(back[2 * samples :])

        yield
        d_pre_out = (d_made * own * (1.0 - tanh_out * tanh_out)).astype(BF)
        d_out[:, here] = d_pre_out
        d_dec[:, here] = (dot(out[...], d_pre_out) * act_slope).astype(BF)
        yield
        loss[:, 0:LANES] += lost

    loop((pairs[0] * 2, pairs[1] * 2), step, hooks, per)


def latent_back(pairs, dec, d_dec, mask, slope, d_latent, hooks=()):
    width = d_dec.shape[0]

    def step(pair):
        here = lanes(pair, WIDE)
        back = dot(dec[...], d_dec[:, here])
        yield
        joined = after(back[:width]) + back[width : 2 * width] + before(back[2 * width :])
        joined = joined.astype(BF).astype(F32) * mask[:, here]
        d_latent[:, here] = (joined - slope[:, here].astype(F32)).astype(BF)

    loop(pairs, step, hooks, 2)


def local_kernel(
    aud, lens, codes, disc, score, spec, spec_t, enc, dec, out, books,
    g_enc, g_dec, g_out, g_books, loss_out,
    pad, ipad, crow, mask, sig, disc_t, score_col, feat_real, mag_real,
    books_t, quant, hidden, enc_t, slope, dec_t, out_t, d_out, d_dec, loss,
):
    clip_count = aud.shape[0]
    pairs = (0, clip_count * LANES // WIDE)
    side = lax.axis_index("grp")
    loss[...] = jnp.zeros_like(loss)
    disc_t[...] = jnp.transpose(disc[...])
    score_col[...] = jnp.transpose(jnp.broadcast_to(score[...], (128, score.shape[1])))
    load_signal(
        clip_count, side, lambda clip: aud.at[clip], lambda clip: None, lens, codes, pad, ipad,
        crow, mask, sig,
    )
    real_side(pairs, sig, disc_t, spec_t, feat_real, mag_real)
    for group in range(2):
        books_t[group] = jnp.transpose(books[group])
    enc_t[...] = jnp.transpose(enc[...])
    dec_t[...] = jnp.transpose(dec[...])
    out_t[...] = jnp.transpose(out[...])
    encode(pairs, enc_t, sig, slope)
    pick(pairs, crow, mask, books_t, quant, slope, loss)

    def book_step(which, carry):
        rows = pl.ds(pl.multiple_of(which // 2 * 256, 256), 256)
        g_books[which] = book_grad(clip_count, crow, slope, which, rows)
        return carry

    lax.fori_loop(0, 4, book_step, 0)
    decode(
        pairs,
        (quant, dec_t, out, out_t, mask, sig, spec, spec_t, disc, disc_t, score_col,
         feat_real, mag_real, hidden, d_out, d_dec),
        loss,
    )
    g_out[...] = dot_nt(hidden[...], d_out[...])

    width = quant.shape[0]
    for part, shift in enumerate((before, lambda values: values, after)):
        g_dec[part * width : (part + 1) * width, :] = dot_nt(shift(quant[...]), d_dec[...])
    latent_back(pairs, dec, d_dec, mask, slope, hidden)

    samples = sig.shape[0]
    for part, shift in enumerate((before, lambda values: values, after)):
        g_enc[part * samples : (part + 1) * samples, :] = dot_nt(shift(sig[...]), hidden[...])
    loss_out[...] = loss[...]


def local_call(audio_t, lengths, codes, disc, score, enc, dec, out, books):
    clip_count, samples, _ = audio_t.shape
    width = disc.shape[1]
    total = clip_count * LANES
    table = spectral_table(samples)
    vmem = pl.BlockSpec(memory_space=pltpu.VMEM)
    smem = pl.BlockSpec(memory_space=pltpu.SMEM)
    return pl.pallas_call(
        local_kernel,
        out_shape=(
            jax.ShapeDtypeStruct((3 * samples, width), F32),
            jax.ShapeDtypeStruct((3 * width, width), F32),
            jax.ShapeDtypeStruct((width, samples), F32),
            jax.ShapeDtypeStruct((4, CB, width // 2), F32),
            jax.ShapeDtypeStruct((1, WIDE), F32),
        ),
        in_specs=[vmem, smem] + [vmem] * 9,
        out_specs=[vmem] * 5,
        scratch_shapes=[
            pltpu.VMEM((samples, LANES), BF),
            pltpu.VMEM((8, LANES), jnp.int32),
            pltpu.VMEM((8, total), jnp.int32),
            pltpu.VMEM((1, total), F32),
            pltpu.VMEM((samples, total), BF),
            pltpu.VMEM((width, 3 * samples), BF),
            pltpu.VMEM((width, 128), F32),
            pltpu.VMEM((width, total), BF),
            pltpu.VMEM((samples // 2, total), F32),
            pltpu.VMEM((2, width // 2, 2 * CB), BF),
            pltpu.VMEM((width, total), BF),
            pltpu.VMEM((width, total), BF),
            pltpu.VMEM((width, 3 * samples), BF),
            pltpu.VMEM((width, total), BF),
            pltpu.VMEM((width, 3 * width), BF),
            pltpu.VMEM((samples, width), BF),
            pltpu.VMEM((samples, total), BF),
            pltpu.VMEM((width, total), BF),
            pltpu.VMEM((1, WIDE), F32),
        ],
        compiler_params=pltpu.CompilerParams(vmem_limit_bytes=56 << 20),
        name="train_local",
    )(
        audio_t, lengths, codes, disc, score.reshape(1, width),
        jnp.asarray(table, BF), jnp.asarray(table.T, BF), enc, dec, out, books,
    )


def shards(
    audio, lengths, codes, disc_weight, disc_score, params, params_mom, params_avg, books,
    books_mom, books_avg,
):
    clip_count, slot_count, samples = audio.shape
    width = disc_weight.shape[1]
    half_width = width // 2
    side = lax.axis_index("grp")
    shared = lax.all_gather(params.astype(BF), "dp", axis=0, tiled=True)
    table = lax.all_gather(books.astype(BF), ("grp", "dp"), axis=1, tiled=True)
    enc_size = 3 * samples * width
    dec_size = 3 * width * width
    enc_weight = shared[:enc_size].reshape(3 * samples, width)
    dec_weight = shared[enc_size : enc_size + dec_size].reshape(3 * width, width)
    out_weight = shared[enc_size + dec_size :].reshape(width, samples)
    codebook = table.reshape(2, 2 * CB, half_width)
    local_count = jnp.sum(
        lax.dynamic_slice_in_dim(lengths, side * clip_count, clip_count, 0)
    ).astype(F32)
    frame_count = lax.psum(local_count, ("dp", "grp"))
    grad_enc, grad_dec, grad_out, grad_book, lost = local_call(
        jnp.swapaxes(audio, 1, 2), lengths, codes, disc_weight, disc_score,
        enc_weight, dec_weight, out_weight, codebook,
    )
    grad_shared = jnp.concatenate(
        [grad_enc.reshape(-1), grad_dec.reshape(-1), grad_out.reshape(-1)]
    )
    grad_shared = lax.psum(grad_shared.astype(BF), "grp").astype(F32)
    grad_book = lax.psum_scatter(
        grad_book.reshape(2, -1), "grp", scatter_dimension=0, tiled=True
    )
    shared_part = lax.psum_scatter(grad_shared, "dp", scatter_dimension=0, tiled=True)
    book_part = lax.psum_scatter(grad_book, "dp", scatter_dimension=1, tiled=True)
    loss_sum = lax.psum(jnp.sum(lost), ("dp", "grp"))
    all_clips = clip_count * lax.axis_size("dp") * lax.axis_size("grp")
    root = math.sqrt(131.0 * all_clips)
    shard_length = params.shape[0]
    spots = lax.axis_index("dp") * shard_length + jnp.arange(shard_length)
    rate = (
        jnp.where(spots < enc_size, 0.65, jnp.where(spots < enc_size + dec_size, 0.14, 0.2)) * root
    )
    shared_grad = shared_part / frame_count
    mom_new = MOMENTUM * params_mom + shared_grad
    param_new = params - rate * (shared_grad + MOMENTUM * mom_new)
    avg_new = AVERAGE * params_avg + (1.0 - AVERAGE) * param_new
    book_rate = 3.9 * math.sqrt(131.0 * all_clips * CB)
    book_grad_mean = book_part / frame_count
    book_mom_new = MOMENTUM * books_mom + book_grad_mean
    book_new = books - book_rate * (book_grad_mean + MOMENTUM * book_mom_new)
    book_avg_new = AVERAGE * books_avg + (1.0 - AVERAGE) * book_new
    return (
        param_new, mom_new, avg_new, book_new, book_mom_new, book_avg_new, loss_sum, frame_count,
    )


MESH = pl.DeviceIdType.MESH
ENC_RATE, DEC_RATE, OUT_RATE, BOOK_RATE = 0.65, 0.14, 0.2, 3.9
CHIPS = (4, 2, 2)
SENDS, ARRIVALS = 16, 72
WAVES = 2


def cols(index, width=128):
    return slice(index * width, (index + 1) * width)


def unflatten_out(flat, square):
    count = square.shape[1] // 2
    left = lax.broadcasted_iota(jnp.int32, (count, 128), 1) < 64
    part = [flat[pl.ds(k, count, stride=5), :] for k in range(5)]
    turned = [pltpu.roll(part[k], 64, 1) for k in (2, 3, 4)]
    even = part[:3]
    odd = [
        jnp.where(left, turned[0], turned[1]), jnp.where(left, turned[1], turned[2]), turned[2],
    ]
    for k in range(3):
        square[k, pl.ds(0, count, stride=2), :] = even[k]
        square[k, pl.ds(1, count, stride=2), :] = odd[k]


def flatten_out(square, flat):
    count = square.shape[1] // 2
    left = lax.broadcasted_iota(jnp.int32, (count, 128), 1) < 64
    even = [square[k, pl.ds(0, count, stride=2), :] for k in range(3)]
    odd = [square[k, pl.ds(1, count, stride=2), :] for k in range(3)]
    turned = [pltpu.roll(values, 64, 1) for values in odd]
    part = [
        even[0], even[1], jnp.where(left, even[2], turned[0]),
        jnp.where(left, turned[0], turned[1]), jnp.where(left, turned[1], turned[2]),
    ]
    for k in range(5):
        flat[pl.ds(k, count, stride=5), :] = part[k]


def update_kernel(
    all_clips, enc_chunks, dec_chunks, grad_p, grad_b, totals,
    par, pmom, pavg, bok, bmom, bavg,
    par_new, pmom_new, pavg_new, bok_new, bmom_new, bavg_new, loss, count,
):
    loss[0, 0] = totals[0, 0]
    count[0, 0] = totals[0, 1]
    frames = totals[0:1, 1:2]
    root = math.sqrt(131.0 * all_clips)
    where = lax.axis_index("dp") * par.shape[0] + lax.broadcasted_iota(jnp.int32, par.shape, 0)
    rate = root * jnp.where(
        where < enc_chunks, ENC_RATE,
        jnp.where(where < enc_chunks + dec_chunks, DEC_RATE, OUT_RATE),
    )

    def write(grad, rate, old, mom, avg, new_ref, mom_ref, avg_ref):
        grad = grad[...] / frames
        mom_new = MOMENTUM * mom[...] + grad
        new = old[...] - rate * (grad + MOMENTUM * mom_new)
        new_ref[...] = new
        mom_ref[...] = mom_new
        avg_ref[...] = AVERAGE * avg[...] + (1.0 - AVERAGE) * new

    write(grad_p, rate, par, pmom, pavg, par_new, pmom_new, pavg_new)
    write(grad_b, BOOK_RATE * root * math.sqrt(CB), bok, bmom, bavg, bok_new, bmom_new, bavg_new)


def fused_kernel(
    enc_rows, dec_rows,
    aud, lens, codes, disc, score, spec, spec_t, par, bok, grad_p, grad_b, totals,
    pad, ipad, crow, mask, sig, disc_t, score_col, feat_real, mag_real,
    books_t, quant, hidden, slope, dec_t, out, out_t, d_out, loss,
    weights, land, flat, square, acc_p, stage_p, got_p, acc_b,
    one_b, two_b, three_b, one_p, two_p, three_p,
    last, stat, zstat, waves, send, recv, wave_sem,
):
    clip_count = aud.shape[0]
    width, samples = disc_t.shape[0], sig.shape[0]
    half = width // 2
    pairs = clip_count * LANES // WIDE
    spot = lax.axis_index("dp")
    side = lax.axis_index("grp")
    other = 1 - side
    p_rows = par.shape[0] * 128 // width
    b_rows = bok.shape[0] * 128 // half
    out_rows = weights.shape[0] - enc_rows - dec_rows

    z, y, x = spot // 4, spot // 2 % 2, spot % 2
    mine_first = y + side * (x - y)
    mine_second = x + side * (y - x)

    def unit(level, first, second):
        return 4 * level + (2 - side) * first + (1 + side) * second

    def around(step):
        return (z + step) % 4

    first_dev = (unit(z, 1 - mine_first, mine_second), side)
    second_dev = (unit(z, mine_first, 1 - mine_second), side)
    pair_dev = (spot, other)

    def level_dev(level):
        return (unit(level, mine_first, mine_second), side)

    barrier = pltpu.get_barrier_semaphore()
    near = [first_dev, second_dev, pair_dev] + [level_dev(around(k)) for k in (1, 2, 3)]
    for device in near:
        pl.semaphore_signal(barrier, inc=1, device_id=device, device_id_type=MESH)

    def wave_copy(clip, slot):
        return pltpu.make_async_copy(aud.at[clip], waves.at[slot], wave_sem.at[slot])

    for slot in range(WAVES):
        wave_copy(slot, slot).start()
    taken = {"send": 0, "recv": 0}

    def take(kind, count=1):
        taken[kind] += count
        return taken[kind] - count

    def copy_to(device, src, dst, send_at, recv_at):
        return pltpu.make_async_remote_copy(
            src_ref=src, dst_ref=dst, send_sem=send.at[send_at], recv_sem=recv.at[recv_at],
            device_id=device, device_id_type=MESH,
        )

    def block(ref, rows, which):
        return ref.at[pl.ds(pl.multiple_of(which * rows, 16), rows), :]

    def p_view(which, count=1):
        rows = pl.ds(pl.multiple_of(which * p_rows, 16), count * p_rows)
        return weights.at[rows, lanes(side, half)]

    def b_view(which, count=1):
        rows = pl.ds(pl.multiple_of(which * b_rows, 16), count * b_rows)
        return land.at[side, rows, :]

    def held(span, which, run):
        if span is None:
            run()
        else:
            pl.when((which >= span[0]) & (which < span[1]))(run)

    def wait_sent(ref, at):
        copy_to(pair_dev, ref, ref, at, 0).wait_send()

    def wait_got(ref, at):
        copy_to(pair_dev, ref, ref, 0, at).wait_recv()

    class Slots:
        def __init__(self):
            self.sent = take("send")
            self.got = take("recv", 15)

    class Gather:
        def __init__(self, view, span, slots):
            self.view, self.span, self.slots = view, span, slots
            self.swap_sent, self.swap_got = take("send"), take("recv")

            def make(slot, which, device):
                return copy_to(
                    device, view(which), view(which), slots.sent, slots.got + slot
                )

            self.levels, self.firsts, self.seconds = [], [], []
            for k in range(4):
                here = unit(around(4 - k), mine_first, mine_second)
                there = unit(around(4 - k), 1 - mine_first, mine_second)
                if k:
                    self.levels.append(make(k - 1, spot, level_dev(around(k))))
                self.firsts.append(make(3 + k, here, first_dev))
                self.seconds.append(
                    [make(7 + 2 * k, here, second_dev), make(8 + 2 * k, there, second_dev)]
                )

        def swap(self, which):
            copy_to(
                pair_dev, self.view(which), self.view(which), self.swap_sent, self.swap_got
            ).start()

        def start(self):
            def run():
                for copy in self.levels + [self.firsts[0], self.seconds[0][0]]:
                    copy.start()
                self.swap(spot)

            held(self.span, spot, run)

        def step(self):
            for k in (1, 2, 3):
                which = unit(around(4 - k), mine_first, mine_second)

                def run(k=k, which=which):
                    self.levels[k - 1].wait_recv()
                    self.firsts[k].start()
                    self.seconds[k][0].start()
                    self.swap(which)

                held(self.span, which, run)

        def back(self, ks):
            for k in ks:
                which = unit(around(4 - k), 1 - mine_first, mine_second)

                def run(k=k, which=which):
                    self.firsts[k].wait_recv()
                    self.seconds[k][1].start()
                    self.swap(which)

                held(self.span, which, run)

        def finish(self, ks):
            for k in ks:
                for slot, first in enumerate((mine_first, 1 - mine_first)):
                    which = unit(around(4 - k), first, 1 - mine_second)

                    def run(k=k, slot=slot, which=which):
                        self.seconds[k][slot].wait_recv()
                        self.swap(which)

                    held(self.span, which, run)

        def settle(self):
            wait_got(self.view(*self.span_units()), self.swap_got)
            wait_sent(self.view(*self.span_units()), self.swap_sent)

        def span_units(self):
            start, stop = self.span or (0, 16)
            return start, stop - start

    class Scatter:
        def __init__(self, span, rows, acc, stage, got, landed, slots):
            self.span, self.rows, self.acc, self.stage, self.got = span, rows, acc, stage, got
            self.landed, self.slots = landed, slots
            start, stop = span or (0, 16)
            self.levels = list(range(start // 4, (stop + 3) // 4))
            both_rows = pl.ds(start * rows, (stop - start) * rows)
            self.pair = copy_to(
                pair_dev, stage.at[both_rows, :], got.at[both_rows, :], take("send"), take("recv")
            )
            one, two, three = landed
            self.sent_one, self.kept_one, self.sent_two, self.kept_two = [], [], [], []
            for level in self.levels:
                for first in range(2):
                    slot = 2 * level + first
                    which = unit(level, first, 1 - mine_second)
                    self.sent_one.append((which, copy_to(
                        second_dev, block(stage, rows, which), one.at[slot],
                        slots.sent, slots.got + slot,
                    )))
                    self.kept_one.append((unit(level, first, mine_second), one, slot))
                which = unit(level, 1 - mine_first, mine_second)
                self.sent_two.append((which, copy_to(
                    first_dev, block(stage, rows, which), two.at[level],
                    slots.sent, slots.got + 8 + level,
                )))
                self.kept_two.append((unit(level, mine_first, mine_second), two, level))

        def read(self, ref, which):
            return ref[pl.ds(pl.multiple_of(which * self.rows, 16), self.rows), :]

        def put(self, ref, which, values):
            ref[pl.ds(pl.multiple_of(which * self.rows, 16), self.rows), :] = values

        def round_one(self):
            self.pair.wait()
            for which, copy in self.sent_one:
                def run(which=which, copy=copy):
                    total = self.read(self.acc, which) + self.read(self.got, which).astype(F32)
                    self.put(self.stage, which, total.astype(BF))
                    copy.start()

                held(self.span, which, run)
            for which, _, _ in self.kept_one:
                def keep(which=which):
                    total = self.read(self.acc, which) + self.read(self.got, which).astype(F32)
                    self.put(self.acc, which, total)

                held(self.span, which, keep)

        def fold(self, kept, sent):
            for (which, landed, slot), (_, copy) in zip(kept, sent):
                def run(which=which, landed=landed, slot=slot, copy=copy):
                    copy.wait_recv()
                    self.put(
                        self.acc, which, self.read(self.acc, which) + landed[slot].astype(F32)
                    )

                held(self.span, which, run)

        def round_two(self):
            self.fold(self.kept_one, self.sent_one)
            for which, copy in self.sent_two:
                def run(which=which, copy=copy):
                    self.put(self.stage, which, self.read(self.acc, which).astype(BF))
                    copy.start()

                held(self.span, which, run)

        def round_three(self):
            self.fold(self.kept_two, self.sent_two)
            for level in self.levels:
                which = unit(level, mine_first, mine_second)
                slot = (z + 7 - level) % 4 % 3

                def run(level=level, which=which, slot=slot):
                    self.put(self.stage, which, self.read(self.acc, which).astype(BF))
                    copy_to(
                        level_dev(level), block(self.stage, self.rows, which),
                        self.landed[2].at[slot], self.slots.sent, self.slots.got + 12 + slot,
                    ).start()

                pl.when(z != level)(functools.partial(held, self.span, which, run))

        def settle(self):
            def run():
                total = self.read(self.acc, spot)
                for slot in range(3):
                    wait_got(self.landed[2].at[slot], self.slots.got + 12 + slot)
                    total = total + self.landed[2][slot].astype(F32)
                self.put(self.acc, spot, total)

            held(self.span, spot, run)

        def drain(self):
            wait_sent(self.stage.at[0 : 15 * self.rows, :], self.slots.sent)

    for j in range(2):
        spots = pl.ds(pl.multiple_of(side * half + j * 128, 128), 128)
        weights[pl.ds(pl.multiple_of(spot * p_rows, 16), p_rows), spots] = par[
            pl.ds(2 * side + j, p_rows, stride=4), :
        ].astype(BF)
        land[side, pl.ds(pl.multiple_of(spot * b_rows, 16), b_rows), cols(j)] = bok[
            pl.ds(j, b_rows, stride=2), :
        ].astype(BF)
    slots_b, slots_p = Slots(), Slots()
    gather_b = Gather(b_view, None, slots_b)
    gather_p, gather_q = Gather(p_view, (0, 6), slots_p), Gather(p_view, (6, 16), slots_p)
    pl.semaphore_wait(barrier, len(near))
    gather_p.start()
    gather_b.start()
    gather_q.start()
    loss[...] = jnp.zeros_like(loss)
    disc_t[...] = jnp.transpose(disc[...])
    score_col[...] = jnp.transpose(jnp.broadcast_to(score[...], (128, score.shape[1])))

    def fetch(clip):
        wave_copy(clip, clip % WAVES).wait()
        return waves.at[clip % WAVES]

    def free(clip):
        @pl.when(clip + WAVES < clip_count)
        def _():
            wave_copy(clip + WAVES, clip % WAVES).start()

    def both(*steps):
        def run():
            for step in steps:
                step()

        return run

    part = functools.partial
    early, late, every = (0,), (1, 2, 3), (0, 1, 2, 3)
    load_signal(
        clip_count, side, fetch, free, lens, codes, pad, ipad, crow, mask, sig,
        {7: both(part(gather_p.back, early), part(gather_b.back, early), part(gather_q.back, early))},
    )
    real_side(
        (0, pairs), sig, disc_t, spec_t, feat_real, mag_real,
        {3: gather_p.step, 4: gather_b.step, 5: part(gather_p.back, late)},
    )
    gather_q.step()
    gather_b.back(late)
    gather_p.finish(every)
    gather_p.settle()
    enc = weights.at[0:enc_rows, :]
    dec = weights.at[enc_rows : enc_rows + dec_rows, :]
    enc_t = dec_t.at[:, 0:enc_rows]
    enc_t[...] = jnp.transpose(enc[...])
    encode(
        (0, pairs), enc_t, sig, slope,
        {0: part(gather_q.back, late), 2: part(gather_b.finish, every)},
    )
    gather_b.settle()
    for group in range(2):
        books_t[group] = jnp.transpose(land[group])
    wait_sent(b_view(0, 15), slots_b.sent)
    pick(
        (0, pairs), crow, mask, books_t, quant, slope, loss,
        {0: part(gather_q.finish, every)},
    )

    d_dec = feat_real
    stage_b, got_b = land.at[0], land.at[1]
    scatter_b = Scatter(None, b_rows, acc_b, stage_b, got_b, (one_b, two_b, three_b), Slots())

    def far_books(level, carry):
        rows = pl.ds(pl.multiple_of(other * half, half), half)
        values = book_grad(clip_count, crow, slope, 2 * other + level, rows)
        stage_b[lanes(level, CB), :] = values.astype(BF)
        return carry

    def near_books(level, carry):
        rows = pl.ds(pl.multiple_of(side * half, half), half)
        acc_b[lanes(level, CB), :] = book_grad(clip_count, crow, slope, 2 * side + level, rows)
        return carry

    lax.fori_loop(0, 2, far_books, 0)
    gather_q.settle()
    scatter_b.pair.start()
    lax.fori_loop(0, 2, near_books, 0)
    wait_sent(p_view(0, 15), slots_p.sent)
    scatter_b.round_one()

    dec_t[...] = jnp.transpose(dec[...])
    for j in range(4):
        flat[pl.ds(j, out_rows, stride=4), :] = weights[
            enc_rows + dec_rows :, cols(j)
        ].astype(F32)
    unflatten_out(flat, square)
    edges = [(k, k * 128, min(k * 128 + 128, samples)) for k in range(3)]
    for k, start, stop in edges:
        out[:, start:stop] = square[k, :, 0 : stop - start].astype(BF)
    out_t[...] = jnp.transpose(out[...])
    decode_refs = (
        quant, dec_t, out, out_t, mask, sig, spec, spec_t, disc, disc_t, score_col,
        feat_real, mag_real, hidden, d_out, d_dec,
    )
    decode(
        (0, pairs), decode_refs, loss, {3: scatter_b.round_two, 7: scatter_b.round_three}, 3
    )

    far_rows = pl.ds(pl.multiple_of(other * half, half), half)
    near_rows = pl.ds(pl.multiple_of(side * half, half), half)
    turned = dec_t

    def shifted_grads(values, low, grad):
        count, span = values.shape[0], turned.shape[1]
        for k, shift in enumerate((before, None, after)):
            far, near = 0.0, 0.0
            for start in range(0, values.shape[1], span):
                here = slice(start, start + span)
                left = values.at[:, here]
                if shift is not None:
                    left = turned.at[0:count, :]
                    left[...] = shift(values[:, here])
                far += dot_nt(left[...], grad[far_rows, here])
                near += dot_nt(left[...], grad[near_rows, here])
            rows = slice(low + k * count, low + (k + 1) * count)
            stage_p[rows, :] = far.astype(BF)
            acc_p[rows, :] = near

    landed, slots = (one_p, two_p, three_p), Slots()
    scatter_d = Scatter((6, 14), p_rows, acc_p, stage_p, got_p, landed, slots)
    scatter_e = Scatter((0, 6), p_rows, acc_p, stage_p, got_p, landed, slots)
    scatter_o = Scatter((14, 16), p_rows, acc_p, stage_p, got_p, landed, slots)
    shifted_grads(quant, enc_rows, d_dec)
    scatter_d.pair.start()
    scatter_b.settle()
    scatter_b.drain()

    valid = jnp.sum(mask[...])
    lost = jnp.sum(loss[...])
    first_lane = lax.broadcasted_iota(jnp.int32, (8, 128), 1) == 0
    stat[0] = jnp.where(first_lane, lost, valid)
    swaps = [
        copy_to(device, stat.at[2 * k], stat.at[2 * k + 1], take("send"), take("recv"))
        for k, device in enumerate((pair_dev, first_dev, second_dev))
    ]
    level_sent, level_got = take("send"), take("recv")
    swaps[0].start()

    def stat_two():
        swaps[0].wait()
        stat[2] = stat[0] + stat[1]
        swaps[1].start()

    def stat_three():
        swaps[1].wait()
        stat[4] = stat[2] + stat[3]
        swaps[2].start()

    latent_back(
        (0, pairs), dec, d_dec, mask, slope, slope,
        {
            0: scatter_d.round_one,
            1: stat_two,
            3: stat_three,
            5: scatter_d.round_two,
        },
    )
    swaps[2].wait()
    zstat[z] = stat[4] + stat[5]
    for k in (1, 2, 3):
        copy_to(level_dev(around(k)), zstat.at[z], zstat.at[z], level_sent, level_got).start()
    shifted_grads(sig, 0, slope)
    scatter_e.pair.start()
    grad_out = dot_nt(hidden[...], d_out[...])
    for k, start, stop in edges:
        square[k, :, 0 : stop - start] = grad_out[:, start:stop]
    scatter_e.round_one()
    flatten_out(square, flat)
    low = enc_rows + dec_rows
    for j in range(2):
        near_part = flat[pl.ds(2 * side + j, out_rows, stride=4), :]
        far_part = flat[pl.ds(2 * other + j, out_rows, stride=4), :]
        acc_p[low : low + out_rows, cols(j)] = near_part
        stage_p[low : low + out_rows, cols(j)] = far_part.astype(BF)
    scatter_o.pair.start()
    scatter_d.round_three()
    wait_got(zstat.at[0:3], level_got)
    wait_sent(zstat.at[0:3], level_sent)
    totals[...] = (zstat[0] + zstat[1]) + (zstat[2] + zstat[3])
    own_b = pl.ds(pl.multiple_of(spot * b_rows, 16), b_rows)
    for j in range(2):
        grad_b[pl.ds(j, b_rows, stride=2), :] = acc_b[own_b, cols(j)]
    scatter_e.round_two()
    scatter_o.round_one()
    scatter_d.settle()
    scatter_e.round_three()
    scatter_o.round_two()
    scatter_e.settle()
    scatter_o.round_three()
    scatter_o.settle()

    own_p = pl.ds(pl.multiple_of(spot * p_rows, 16), p_rows)
    swap = copy_to(pair_dev, acc_p.at[own_p, :], last, take("send"), take("recv"))
    swap.start()
    for j in range(2):
        grad_p[pl.ds(2 * side + j, p_rows, stride=4), :] = acc_p[own_p, cols(j)]
    scatter_e.drain()
    swap.wait()
    for j in range(2):
        grad_p[pl.ds(2 * other + j, p_rows, stride=4), :] = last[:, cols(j)]
    assert taken == {"send": SENDS, "recv": ARRIVALS}, taken


def fused(
    audio, lengths, codes, disc_weight, disc_score, params, params_mom, params_avg, books,
    books_mom, books_avg,
):
    clip_count, _, samples = audio.shape
    width = disc_weight.shape[1]
    half = width // 2
    chips = lax.axis_size("dp")
    total = clip_count * LANES
    table = spectral_table(samples)
    p_rows, b_rows = params.shape[0] // width, books.shape[1] // half
    all_rows, book_rows = p_rows * chips, b_rows * chips
    vmem = pl.BlockSpec(memory_space=pltpu.VMEM)
    smem = pl.BlockSpec(memory_space=pltpu.SMEM)
    p_shape = (params.shape[0] // 128, 128)
    b_shape = (books.shape[1] // 128, 128)
    all_clips = clip_count * chips * lax.axis_size("grp")
    weights = [value.reshape(p_shape) for value in (params, params_mom, params_avg)]
    tables = [value.reshape(b_shape) for value in (books, books_mom, books_avg)]
    grad_shapes = [jax.ShapeDtypeStruct(p_shape, F32), jax.ShapeDtypeStruct(b_shape, F32)]
    grads = pl.pallas_call(
        functools.partial(fused_kernel, 3 * samples, 3 * width),
        out_shape=grad_shapes + [jax.ShapeDtypeStruct((8, 128), F32)],
        in_specs=[pl.BlockSpec(memory_space=pl.ANY), smem] + [vmem] * 7,
        out_specs=[vmem] * 3,
        scratch_shapes=[
            pltpu.VMEM((samples, LANES), BF),
            pltpu.VMEM((8, LANES), jnp.int32),
            pltpu.VMEM((8, total), jnp.int32),
            pltpu.VMEM((1, total), F32),
            pltpu.VMEM((samples, total), BF),
            pltpu.VMEM((width, 3 * samples), BF),
            pltpu.VMEM((width, 128), F32),
            pltpu.VMEM((width, total), BF),
            pltpu.VMEM((samples // 2, total), F32),
            pltpu.VMEM((2, half, 2 * CB), BF),
            pltpu.VMEM((width, total), BF),
            pltpu.VMEM((width, total), BF),
            pltpu.VMEM((width, total), BF),
            pltpu.VMEM((width, 3 * width), BF),
            pltpu.VMEM((width, samples), BF),
            pltpu.VMEM((samples, width), BF),
            pltpu.VMEM((samples, total), BF),
            pltpu.VMEM((1, WIDE), F32),
            pltpu.VMEM((all_rows, width), BF),
            pltpu.VMEM((2, book_rows, half), BF),
            pltpu.VMEM((width * samples // 128, 128), F32),
            pltpu.VMEM((3, width, 128), F32),
            pltpu.VMEM((all_rows, half), F32),
            pltpu.VMEM((all_rows, half), BF),
            pltpu.VMEM((all_rows, half), BF),
            pltpu.VMEM((book_rows, half), F32),
            pltpu.VMEM((8, b_rows, half), BF),
            pltpu.VMEM((4, b_rows, half), BF),
            pltpu.VMEM((3, b_rows, half), BF),
            pltpu.VMEM((8, p_rows, half), BF),
            pltpu.VMEM((4, p_rows, half), BF),
            pltpu.VMEM((3, p_rows, half), BF),
            pltpu.VMEM((p_rows, half), F32),
            pltpu.VMEM((6, 8, 128), F32),
            pltpu.VMEM((4, 8, 128), F32),
            pltpu.VMEM((WAVES, samples, audio.shape[1]), BF),
            pltpu.SemaphoreType.DMA((SENDS,)),
            pltpu.SemaphoreType.DMA((ARRIVALS,)),
            pltpu.SemaphoreType.DMA((WAVES,)),
        ],
        compiler_params=pltpu.CompilerParams(
            vmem_limit_bytes=VMEM_LIMIT, collective_id=0, has_side_effects=True
        ),
        name="train_step",
    )(
        jnp.swapaxes(audio, 1, 2), lengths, codes, disc_weight, disc_score.reshape(1, width),
        jnp.asarray(table, BF), jnp.asarray(table.T, BF), weights[0], tables[0],
    )
    outs = pl.pallas_call(
        functools.partial(
            update_kernel, all_clips, 3 * samples * width // 128, 3 * width * width // 128
        ),
        out_shape=[grad_shapes[0]] * 3 + [grad_shapes[1]] * 3
        + [jax.ShapeDtypeStruct((1, 1), F32)] * 2,
        in_specs=[vmem] * 9,
        out_specs=[vmem] * 6 + [smem] * 2,
        name="train_update",
    )(*grads, *weights, *tables)
    return (
        *(value.reshape(params.shape) for value in outs[:3]),
        *(value.reshape(books.shape) for value in outs[3:6]),
        outs[6].reshape(()),
        outs[7].reshape(()),
    )


def solution(mesh):
    in_specs = (
        P(("dp", "grp"), None, None), P("dp"), P(None, None, "dp", None), P(), P(), P("dp"),
        P("dp"), P("dp"), P("grp", "dp"), P("grp", "dp"), P("grp", "dp"),
    )
    out_specs = (
        P("dp"), P("dp"), P("dp"), P("grp", "dp"), P("grp", "dp"), P("grp", "dp"), P(), P(),
    )
    body = fused if mesh.shape["dp"] == math.prod(CHIPS) else shards
    return jax.shard_map(body, mesh=mesh, in_specs=in_specs, out_specs=out_specs, check_vma=False)
```
